512 devices in a mesh: rep: 64 (over y, z_hi, x), fsdp: 8 (over z_lo, core).
Axes of the slice: x: 4, y: 8, z: 8 (z_hi: 2, z_lo: 4; z = z_hi * 4 + z_lo), core: 2. Of those that a mesh axis runs over, the one named last changes fastest.
Arguments:
- tokens: bfloat16 [65536, 8192], P(('rep', 'fsdp')), may hold values from -6 to 6
- cotangent: bfloat16 [65536, 512], P(('rep', 'fsdp')), may hold values from -6 to 6
- local_weights: bfloat16 [64, 8192, 512], P('rep', 'fsdp'), may hold values from -16 to 16
- anchor: float32 [8, 1024, 512], P('fsdp', 'rep'), may hold values from -6 to 6
- momentum: float32 [8, 1024, 512], P('fsdp', 'rep'), may hold values from -3 to 3
Outputs:
- mixed: bfloat16 [64, 8192, 512], P('rep', 'fsdp')
- new_anchor: float32 [8, 1024, 512], P('fsdp', 'rep')
- new_momentum: float32 [8, 1024, 512], P('fsdp', 'rep')
The draws below stay inside these ranges and needn't reach their ends.
All inputs are finite; a program needn't handle non-finite values.
Results may differ from the reference program's by a relative error of at most 0.0085.
Values may be sent and summed in bfloat16 or wider, within the bound.
No kernel may reach another device: no remote copies, remote signals or barrier semaphores. Data moves between devices by JAX's collectives and lax.ppermute only.
A program may use at most 64 MiB of HBM per device.

```python
import jax
import jax.numpy as jnp
from jax import lax

D = 8192
HD = 128
E = 512
TOK_DEV = 128
TOKENS = 65536
N_REP = 64
N_FSDP = 8


def raised(result, own_key, source, target, blocks, factor):
    owner, partner = [(jnp.arange(result.shape[dim]) // (result.shape[dim] // blocks)).reshape([-1 if axis == dim else 1 for axis in range(result.ndim)]) for dim in (source, target)]
    chosen = jax.random.permutation(own_key, blocks)[partner]
    strong = (owner == chosen) | (owner == (partner + blocks // 2) % blocks)
    return jnp.where(strong, factor * result, result)


def levels(stream_key, dims, pieces, least, high):
    gain, own = 1.0, jax.random.fold_in(stream_key, 6)
    for dim, parts in pieces:
        steps = jnp.exp(jax.random.uniform(jax.random.fold_in(own, dim), (parts,), jnp.float32, least / len(pieces), high / len(pieces)))
        gain = gain * jnp.repeat(steps, dims[dim] // parts).reshape([-1 if axis == dim else 1 for axis in range(len(dims))])
    return gain


def noise(stream_key, dims, scale, most, pieces=(), kind=jnp.bfloat16):
    factor_of = levels(stream_key, dims, pieces, -0.22, 0.18) if pieces else 1.0
    drawn = jax.random.normal(stream_key, dims, jnp.float32) * scale * factor_of
    return jnp.minimum(jnp.maximum(drawn, -most), most).astype(kind)


def gaussian_with(key, shape, deviation, reach, cuts, heavy, kind=jnp.bfloat16):
    drawn = deviation * jax.random.normal(key, shape, jnp.float32)
    if cuts:
        drawn = drawn * levels(key, shape, cuts, -0.22, 0.18)
    return jnp.clip(raised(drawn, jax.random.fold_in(key, 3), *heavy), -reach, reach).astype(kind)


def setup_inputs(seed: int = 0) -> dict:
    streams_of = jax.random.split(jax.random.key(seed), 6)
    return {
        "tokens": noise(streams_of[0], (TOKENS, D), 1.0, 6.0, ((0, 512),)),
        "cotangent": noise(streams_of[1], (TOKENS, E), 1.0, 6.0, ((0, 512),)),
        "local_weights": gaussian_with(streams_of[2], (N_REP, D, E), 1.0, 16.0, ((0, 64), (1, 8)), (0, 1, 64, 4.0)),
        "anchor": noise(streams_of[3], (N_FSDP, D // N_FSDP, E), 1.0, 6.0, ((0, 8), (1, 64)), jnp.float32),
        "momentum": noise(streams_of[4], (N_FSDP, D // N_FSDP, E), 0.5, 3.0, ((0, 8), (1, 64)), jnp.float32),
    }


EPS = 1e-06
ETA = 1.0
MOMENT = 0.9
OUTER_RATE = 0.7
MIX_RATE = 0.5

def replica_step(rows_in, incoming, weight_now):
    projected = jnp.dot(rows_in, weight_now, preferred_element_type=jnp.float32)
    count = projected.shape[0]
    heads = projected.reshape(count, -1, HD)
    scale = lax.rsqrt(lax.optimization_barrier(jnp.mean(heads * heads, axis=-1, keepdims=True)) + EPS)
    normed = heads * scale
    upstream = incoming.astype(jnp.float32).reshape(count, -1, HD)
    back = scale * (upstream - normed * lax.optimization_barrier(jnp.mean(upstream * normed, axis=-1, keepdims=True)))
    key_grad = back.reshape(count, -1).astype(jnp.bfloat16)
    grad = lax.dot_general(rows_in, key_grad, (((0,), (0,)), ((), ())), preferred_element_type=jnp.float32)
    return (weight_now.astype(jnp.float32) - ETA * grad).astype(jnp.bfloat16)

def reference(tokens, cotangent, local_weights, anchor, momentum):
    rows_rep = TOK_DEV * N_FSDP

    def accumulate(carry, index):
        start = (index * rows_rep).astype(jnp.int32)
        rows_in = lax.dynamic_slice_in_dim(tokens, start, rows_rep, 0)
        incoming = lax.dynamic_slice_in_dim(cotangent, start, rows_rep, 0)
        local = replica_step(rows_in, incoming, local_weights[index])
        return (carry + local.astype(jnp.float32), local)
    total, stacked = lax.scan(accumulate, jnp.zeros((D, E), jnp.float32), jnp.arange(N_REP, dtype=jnp.int32))
    base = anchor.reshape(D, E)
    average = total / N_REP
    delta = base - average
    new_mom = MOMENT * momentum.reshape(D, E) + delta
    new_base = base - OUTER_RATE * (delta + MOMENT * new_mom)

    def blend(local):
        return ((1.0 - MIX_RATE) * local.astype(jnp.float32) + MIX_RATE * new_base).astype(jnp.bfloat16)
    mixed = lax.map(blend, stacked)
    return (mixed, new_base.reshape(N_FSDP, D // N_FSDP, E), new_mom.reshape(N_FSDP, D // N_FSDP, E))
```

```python
import jax
import jax.numpy as jnp
from jax import lax
from jax.experimental import pallas as pl
from jax.experimental.pallas import tpu as pltpu
from jax.sharding import Mesh
from jax.sharding import PartitionSpec as P

HD = 128
EPS = 1e-06
ETA = 1.0
MOMENT = 0.9
OUTER_RATE = 0.7
MIX_RATE = 0.5

AXES = ("y", "zh", "x", "zl", "core")
SIZES = (8, 2, 4, 4, 2)
REP = ("y", "zh", "x")
FSDP = ("zl", "core")
SWAP = [(0, 1), (1, 0)]
BF = jnp.bfloat16
F32 = jnp.float32
LIMIT = 48 * 1024 * 1024


def params():
    return pltpu.CompilerParams(vmem_limit_bytes=LIMIT)


def regroup_kernel(x_ref, out_ref):
    out_ref[0] = x_ref[...]


def regroup(tokens, parts):
    rows, width = tokens.shape
    return pl.pallas_call(
        regroup_kernel,
        grid=(parts,),
        in_specs=[pl.BlockSpec((rows, width // parts), lambda i: (0, i))],
        out_specs=pl.BlockSpec((1, rows, width // parts), lambda i: (i, 0, 0)),
        out_shape=jax.ShapeDtypeStruct((parts, rows, width // parts), tokens.dtype),
        compiler_params=params(),
    )(tokens)


def project_kernel(x_ref, w_ref, out_ref):
    out_ref[0] = jnp.dot(x_ref[0], w_ref[...], preferred_element_type=F32).astype(BF)


def project(x, w):
    n, rows, depth = x.shape
    features = w.shape[1]
    return pl.pallas_call(
        project_kernel,
        grid=(n,),
        in_specs=[
            pl.BlockSpec((1, rows, depth), lambda i: (i, 0, 0)),
            pl.BlockSpec((depth, features), lambda i: (0, 0)),
        ],
        out_specs=pl.BlockSpec((1, rows, features), lambda i: (i, 0, 0)),
        out_shape=jax.ShapeDtypeStruct((n, rows, features), BF),
        compiler_params=params(),
    )(x, w)


def norm_kernel(p_ref, g_ref, out_ref):
    for h in range(g_ref.shape[1] // HD):
        cols = pl.ds(h * HD, HD)
        projected = p_ref[0, :, cols].astype(F32)
        for i in range(1, p_ref.shape[0]):
            projected += p_ref[i, :, cols].astype(F32)
        scale = lax.rsqrt(jnp.mean(projected * projected, axis=-1, keepdims=True) + EPS)
        normed = projected * scale
        upstream = g_ref[:, cols].astype(F32)
        back = scale * (upstream - normed * jnp.mean(upstream * normed, axis=-1, keepdims=True))
        out_ref[:, cols] = back.astype(BF)


def norm_grad(parts, cotangent):
    return pl.pallas_call(
        norm_kernel,
        out_shape=jax.ShapeDtypeStruct(cotangent.shape, BF),
        compiler_params=params(),
    )(parts, cotangent)


def tdot(a, b):
    return lax.dot_general(a, b, (((0,), (0,)), ((), ())), preferred_element_type=F32)


def inner_kernel(core_ref, xs_ref, xo_ref, ks_ref, ko_ref, w_ref, out_ref):
    xs = xs_ref[...].reshape(ks_ref.shape[0], -1)
    grad = tdot(xs, ks_ref[...]) + tdot(xo_ref[...], ko_ref[...])
    out_ref[...] = (w_ref[...].astype(F32) - ETA * grad).astype(BF)


def inner_step(core, x, x_other, k_same, k_other, w, block=256):
    rows, features = w.shape
    n, tokens, _ = x.shape
    steps = rows // block
    half = n * tokens
    return pl.pallas_call(
        inner_kernel,
        grid_spec=pltpu.PrefetchScalarGridSpec(
            num_scalar_prefetch=1,
            grid=(steps,),
            in_specs=[
                pl.BlockSpec((n, tokens, block), lambda i, c: (0, 0, c[0] * steps + i)),
                pl.BlockSpec((half, block), lambda i, c: (0, i)),
                pl.BlockSpec((half, features), lambda i, c: (0, 0)),
                pl.BlockSpec((half, features), lambda i, c: (0, 0)),
                pl.BlockSpec((block, features), lambda i, c: (i, 0)),
            ],
            out_specs=pl.BlockSpec((block, features), lambda i, c: (i, 0)),
        ),
        out_shape=jax.ShapeDtypeStruct((rows, features), BF),
        compiler_params=params(),
    )(core, x, x_other, k_same, k_other, w)


def outer_kernel(l_ref, a_ref, m_ref, base_ref, mom_ref, all_ref):
    n = l_ref.shape[0]
    total = l_ref[0].astype(F32)
    for i in range(1, n):
        total += l_ref[i].astype(F32)
    base = a_ref[0]
    delta = base - total / n
    new_mom = MOMENT * m_ref[0] + delta
    new_base = base - OUTER_RATE * (delta + MOMENT * new_mom)
    mom_ref[0] = new_mom
    base_ref[0] = new_base
    low = new_base.astype(BF)
    for i in range(n):
        all_ref[i] = low


def outer_step(locals_, anchor, momentum):
    return pl.pallas_call(
        outer_kernel,
        out_shape=(
            jax.ShapeDtypeStruct(anchor.shape, F32),
            jax.ShapeDtypeStruct(momentum.shape, F32),
            jax.ShapeDtypeStruct(locals_.shape, BF),
        ),
        compiler_params=params(),
    )(locals_, anchor, momentum)


def mix_kernel(l_ref, b_ref, out_ref):
    mixed = (1.0 - MIX_RATE) * l_ref[...].astype(F32) + MIX_RATE * b_ref[...].astype(F32)
    out_ref[0] = mixed.astype(BF)


def mix(local, base, block=256):
    rows, features = local.shape
    return pl.pallas_call(
        mix_kernel,
        grid=(rows // block,),
        in_specs=[pl.BlockSpec((block, features), lambda i: (i, 0))] * 2,
        out_specs=pl.BlockSpec((1, block, features), lambda i: (0, i, 0)),
        out_shape=jax.ShapeDtypeStruct((1, rows, features), BF),
        compiler_params=params(),
    )(local, base)


def body(tokens, cotangent, local_weights, anchor, momentum):
    own = local_weights[0]
    depth, features = own.shape
    rows = tokens.shape[0]
    chips, n_rep = SIZES[3], SIZES[0] * SIZES[1] * SIZES[2]
    core = lax.axis_index("core")
    x = lax.all_to_all(regroup(tokens, chips), "zl", 0, 0, tiled=True)
    chip_weights = lax.all_gather(own, "core", axis=0, tiled=True)
    parts = project(x, chip_weights)
    send = lax.dynamic_slice_in_dim(x, (1 - core) * depth, depth, 2).reshape(chips * rows, depth)
    x_other = lax.ppermute(send, "core", SWAP)
    mine = lax.all_to_all(parts, "zl", 0, 0, tiled=True)
    key_grad = norm_grad(mine, cotangent)
    spread = jnp.broadcast_to(key_grad[None], (chips, rows, features))
    k_same = lax.all_to_all(spread, "zl", 0, 0, tiled=True).reshape(chips * rows, features)
    k_other = lax.ppermute(k_same, "core", SWAP)
    local = inner_step(core.reshape(1), x, x_other, k_same, k_other, own)
    shares = lax.all_to_all(local.reshape(n_rep, -1, features), REP, 0, 0, tiled=True)
    new_base, new_mom, spread_base = outer_step(shares, anchor, momentum)
    base = lax.all_to_all(spread_base, REP, 0, 0, tiled=True).reshape(depth, features)
    return mix(local, base), new_base, new_mom


def solution(mesh):
    fine = Mesh(mesh.devices.reshape(SIZES), AXES)
    placed = (
        P((*REP, *FSDP), None),
        P((*REP, *FSDP), None),
        P(REP, FSDP, None),
        P(FSDP, REP, None),
        P(FSDP, REP, None),
    )
    return jax.shard_map(
        body,
        mesh=fine,
        in_specs=placed,
        out_specs=(P(REP, FSDP, None), P(FSDP, REP, None), P(FSDP, REP, None)),
        check_vma=False,
    )
```

```python
import jax
import jax.numpy as jnp
from jax import lax
from jax.experimental import pallas as pl
from jax.experimental.pallas import tpu as pltpu
from jax.sharding import Mesh
from jax.sharding import PartitionSpec as P

HD = 128
EPS = 1e-06
ETA = 1.0
MOMENT = 0.9
OUTER_RATE = 0.7
MIX_RATE = 0.5

AXES = ("y", "zh", "x", "zl", "core")
SIZES = (8, 2, 4, 4, 2)
REP = ("y", "zh", "x")
FSDP = ("zl", "core")
SWAP = [(0, 1), (1, 0)]
BF = jnp.bfloat16
F32 = jnp.float32
LIMIT = 48 * 1024 * 1024


def call(kernel, out_shape, flops=0, moved=0, **more):
    return pl.pallas_call(
        kernel,
        out_shape=out_shape,
        compiler_params=pltpu.CompilerParams(vmem_limit_bytes=LIMIT),
        cost_estimate=pl.CostEstimate(flops=flops, bytes_accessed=moved, transcendentals=0),
        **more,
    )


def project_kernel(x_ref, w_ref, out_ref):
    out_ref[...] = jnp.dot(x_ref[...], w_ref[...], preferred_element_type=F32).astype(BF)


def project(x, w):
    rows, depth = x.shape
    features = w.shape[1]
    return call(
        project_kernel,
        jax.ShapeDtypeStruct((rows, features), BF),
        flops=2 * rows * depth * features,
        moved=2 * (x.size + w.size),
    )(x, w)


def norm_kernel(a_ref, b_ref, c_ref, d_ref, g_ref, out_ref):
    for h in range(g_ref.shape[1] // HD):
        cols = pl.ds(h * HD, HD)
        projected = a_ref[:, cols].astype(F32)
        for ref in (b_ref, c_ref, d_ref):
            projected += ref[:, cols].astype(F32)
        scale = lax.rsqrt(jnp.mean(projected * projected, axis=-1, keepdims=True) + EPS)
        normed = projected * scale
        upstream = g_ref[:, cols].astype(F32)
        back = scale * (upstream - normed * jnp.mean(upstream * normed, axis=-1, keepdims=True))
        out_ref[:, cols] = back.astype(BF)


def norm_grad(parts, cotangent):
    return call(
        norm_kernel,
        jax.ShapeDtypeStruct(cotangent.shape, BF),
        moved=6 * cotangent.size * 2,
    )(*parts, cotangent)


def split_kernel(core_ref, x_ref, mine_ref, send_ref):
    depth = mine_ref.shape[0]
    mine = pl.ds(pl.multiple_of(core_ref[0] * depth, depth), depth)
    other = pl.ds(pl.multiple_of((1 - core_ref[0]) * depth, depth), depth)
    mine_ref[...] = x_ref[:, mine].T
    send_ref[...] = x_ref[:, other].T


def split(core, x):
    rows, width = x.shape
    shape = jax.ShapeDtypeStruct((width // 2, rows), BF)
    vmem = pl.BlockSpec(memory_space=pltpu.VMEM)
    return call(
        split_kernel,
        (shape, shape),
        in_specs=[pl.BlockSpec(memory_space=pltpu.SMEM), vmem],
        out_specs=(vmem, vmem),
    )(core.reshape(1), x)


def inner_kernel(*refs):
    *xs, ks_ref, ko_ref, w_ref, out_ref = refs
    x = jnp.concatenate([ref[...] for ref in xs], axis=1)
    k = jnp.concatenate([ks_ref[...], ko_ref[...]], axis=0)
    grad = jnp.dot(x, k, preferred_element_type=F32)
    local = (w_ref[...].astype(F32) - ETA * grad).astype(BF)
    ny, nx, nz, own, _ = out_ref.shape
    for y in range(ny):
        for z in range(nz):
            for x in range(nx):
                start = ((y * nz + z) * nx + x) * own
                out_ref[y, x, z] = local[start : start + own]


def inner_step(xs, k_same, k_other, w, block=256):
    rows, features = w.shape
    half = k_same.shape[0]
    ny, nz, nx = SIZES[:3]
    own = rows // (ny * nz * nx)
    by = block // (nz * nx * own)
    return call(
        inner_kernel,
        jax.ShapeDtypeStruct((ny, nx, nz, own, features), BF),
        flops=4 * rows * half * features,
        moved=4 * (rows * half + w.size + k_same.size),
        grid=(rows // block,),
        in_specs=[pl.BlockSpec((block, x.shape[1]), lambda i: (i, 0)) for x in xs]
        + [
            pl.BlockSpec((half, features), lambda i: (0, 0)),
            pl.BlockSpec((half, features), lambda i: (0, 0)),
            pl.BlockSpec((block, features), lambda i: (i, 0)),
        ],
        out_specs=pl.BlockSpec((by, nx, nz, own, features), lambda i: (i, 0, 0, 0, 0)),
    )(*xs, k_same, k_other, w)


def total_kernel(l_ref, out_ref, low_ref):
    total = l_ref[0].astype(F32)
    for i in range(1, l_ref.shape[0]):
        total += l_ref[i].astype(F32)
    out_ref[...] = total
    low_ref[...] = total.astype(BF)


def half_total(shares):
    shape = shares.shape[1:]
    return call(
        total_kernel,
        (jax.ShapeDtypeStruct(shape, F32), jax.ShapeDtypeStruct(shape, BF)),
        moved=2 * shares.size,
    )(shares)


def outer_kernel(zh_ref, s_ref, o_ref, am_ref, pam_ref, base_ref, mom_ref, all_ref):
    zh = zh_ref[0]
    own = am_ref.shape[1]
    n_rep = SIZES[0] * SIZES[1] * SIZES[2]

    def step(which, held):
        rows = pl.ds(pl.multiple_of(which * own, own), own)
        average = (s_ref[rows] + o_ref[rows].astype(F32)) / n_rep
        base = held[0]
        delta = base - average
        new_mom = MOMENT * held[1] + delta
        return rows, base - OUTER_RATE * (delta + MOMENT * new_mom), new_mom

    rows, new_base, new_mom = step(zh, am_ref)
    base_ref[0] = new_base
    mom_ref[0] = new_mom
    partner_rows, partner_base, _ = step(1 - zh, pam_ref)
    low, partner_low = new_base.astype(BF), partner_base.astype(BF)
    for i in range(all_ref.shape[0]):
        all_ref[i, rows] = low
        all_ref[i, partner_rows] = partner_low


def outer_step(zh, total, other, held, partner_held, n):
    own, features = held.shape[1:]
    vmem = pl.BlockSpec(memory_space=pltpu.VMEM)
    return call(
        outer_kernel,
        (
            jax.ShapeDtypeStruct((1, own, features), F32),
            jax.ShapeDtypeStruct((1, own, features), F32),
            jax.ShapeDtypeStruct((n, *total.shape), BF),
        ),
        moved=2 * n * total.size,
        in_specs=[pl.BlockSpec(memory_space=pltpu.SMEM)] + [vmem] * 4,
        out_specs=(vmem,) * 3,
    )(zh.reshape(1), total, other, held, partner_held)


def mix_kernel(l_ref, b_ref, out_ref):
    mixed = (1.0 - MIX_RATE) * l_ref[...].astype(F32) + MIX_RATE * b_ref[...].astype(F32)
    mixed = mixed.astype(BF)
    ny, nx, nz, own, _ = l_ref.shape
    for y in range(ny):
        for z in range(nz):
            for x in range(nx):
                out_ref[0, pl.ds(((y * nz + z) * nx + x) * own, own)] = mixed[y, x, z]


def mix(local, base, block=2):
    ny, nx, nz, own, features = local.shape
    rows = nx * nz * own
    return call(
        mix_kernel,
        jax.ShapeDtypeStruct((1, ny * rows, features), BF),
        moved=6 * local.size,
        grid=(ny // block,),
        in_specs=[pl.BlockSpec((block, nx, nz, own, features), lambda i: (i, 0, 0, 0, 0))] * 2,
        out_specs=pl.BlockSpec((1, block * rows, features), lambda i: (0, i, 0)),
    )(local, base)


def across(value, k):
    return lax.ppermute(value, "zl", [(i, i ^ k) for i in range(SIZES[3])])


def body(tokens, cotangent, local_weights, anchor, momentum):
    own = local_weights[0]
    depth, features = own.shape
    width = tokens.shape[1] // SIZES[3]
    core, zl, zh = (lax.axis_index(name) for name in ("core", "zl", "zh"))
    chunk = [lax.dynamic_slice_in_dim(tokens, (zl ^ k) * width, width, 1) for k in range(4)]
    chip_weights = lax.all_gather(own, "core", axis=0, tiled=True)
    got = {k: across(chunk[k], k) for k in (3, 2, 1)}
    got[0] = chunk[0]
    held = jnp.concatenate([anchor, momentum], axis=0)
    partner_held = lax.ppermute(held, "zh", SWAP)
    made = project(got[0], chip_weights)
    got[1], made, partner_held = lax.optimization_barrier((got[1], made, partner_held))
    mine, other = {}, {}
    parts = [made]
    for k in (1, 2, 3):
        got[k], parts, other = lax.optimization_barrier((got[k], parts, other))
        parts.append(across(project(got[k], chip_weights), k))
        mine[k - 1], send = split(core, got[k - 1])
        other[k - 1] = lax.ppermute(send, "core", SWAP)
    parts, other = lax.optimization_barrier((parts, other))
    key_grad = norm_grad(parts, cotangent)
    got[3], key_grad = lax.optimization_barrier((got[3], key_grad))
    mine[3], send = split(core, got[3])
    other[3] = lax.ppermute(send, "core", SWAP)
    k_same = jnp.concatenate([key_grad] + [across(key_grad, k) for k in (1, 2, 3)], axis=0)
    k_other = lax.ppermute(k_same, "core", SWAP)
    xs = [mine[k] for k in range(4)] + [other[k] for k in range(4)]
    local = inner_step(xs, k_same, k_other, own)
    ny, nx, nz, rows, _ = local.shape
    shares = lax.all_to_all(local.reshape(ny * nx, nz * rows, features), ("y", "x"), 0, 0, tiled=True)
    total, low = half_total(shares)
    other = lax.ppermute(low, "zh", SWAP)
    new_base, new_mom, spread = outer_step(zh, total, other, held, partner_held, ny * nx)
    base = lax.all_to_all(spread, ("y", "x"), 0, 0, tiled=True).reshape(local.shape)
    return mix(local, base), new_base, new_mom


def solution(mesh):
    fine = Mesh(mesh.devices.reshape(SIZES), AXES)
    placed = (
        P((*REP, *FSDP), None),
        P((*REP, *FSDP), None),
        P(REP, FSDP, None),
        P(FSDP, REP, None),
        P(FSDP, REP, None),
    )
    return jax.shard_map(
        body,
        mesh=fine,
        in_specs=placed,
        out_specs=(P(REP, FSDP, None), P(FSDP, REP, None), P(FSDP, REP, None)),
        check_vma=False,
    )
```

```python
import jax
import jax.numpy as jnp
from jax import lax
from jax.experimental import pallas as pl
from jax.experimental.pallas import tpu as pltpu
from jax.sharding import Mesh
from jax.sharding import PartitionSpec as P

HD = 128
EPS = 1e-06
ETA = 1.0
MOMENT = 0.9
OUTER_RATE = 0.7
MIX_RATE = 0.5

AXES = ("y", "zh", "x", "zl", "core")
SIZES = (8, 2, 4, 4, 2)
REP = ("y", "zh", "x")
FSDP = ("zl", "core")
SWAP = [(0, 1), (1, 0)]
BF = jnp.bfloat16
F32 = jnp.float32
LIMIT = 48 * 1024 * 1024


def call(kernel, out_shape, flops=0, moved=0, **more):
    return pl.pallas_call(
        kernel,
        out_shape=out_shape,
        compiler_params=pltpu.CompilerParams(vmem_limit_bytes=LIMIT),
        cost_estimate=pl.CostEstimate(flops=flops, bytes_accessed=moved, transcendentals=0),
        **more,
    )


def project_kernel(x_ref, w_ref, out_ref):
    out_ref[...] = jnp.dot(x_ref[...], w_ref[...], preferred_element_type=F32).astype(BF)


def project(x, w):
    rows, depth = x.shape
    features = w.shape[1]
    return call(
        project_kernel,
        jax.ShapeDtypeStruct((rows, features), BF),
        flops=2 * rows * depth * features,
        moved=2 * (x.size + w.size),
    )(x, w)


def norm_kernel(a_ref, b_ref, c_ref, d_ref, g_ref, out_ref):
    for h in range(g_ref.shape[1] // HD):
        cols = pl.ds(h * HD, HD)
        projected = a_ref[:, cols].astype(F32)
        for ref in (b_ref, c_ref, d_ref):
            projected += ref[:, cols].astype(F32)
        scale = lax.rsqrt(jnp.mean(projected * projected, axis=-1, keepdims=True) + EPS)
        normed = projected * scale
        upstream = g_ref[:, cols].astype(F32)
        back = scale * (upstream - normed * jnp.mean(upstream * normed, axis=-1, keepdims=True))
        out_ref[:, cols] = back.astype(BF)


def norm_grad(parts, cotangent):
    return call(
        norm_kernel,
        jax.ShapeDtypeStruct(cotangent.shape, BF),
        moved=6 * cotangent.size * 2,
    )(*parts, cotangent)


def split_kernel(core_ref, x_ref, mine_ref, send_ref):
    depth = mine_ref.shape[0]
    mine = pl.ds(pl.multiple_of(core_ref[0] * depth, depth), depth)
    other = pl.ds(pl.multiple_of((1 - core_ref[0]) * depth, depth), depth)
    mine_ref[...] = x_ref[:, mine].T
    send_ref[...] = x_ref[:, other].T


def split(core, x):
    rows, width = x.shape
    shape = jax.ShapeDtypeStruct((width // 2, rows), BF)
    vmem = pl.BlockSpec(memory_space=pltpu.VMEM)
    return call(
        split_kernel,
        (shape, shape),
        in_specs=[pl.BlockSpec(memory_space=pltpu.SMEM), vmem],
        out_specs=(vmem, vmem),
    )(core.reshape(1), x)


def inner_kernel(x_ref, *refs):
    *xs, ks_ref, ko_ref, w_ref, out0, out1, out2, out3, held_ref = refs
    x = jnp.concatenate([ref[...] for ref in xs], axis=1)
    k = jnp.concatenate([ks_ref[...], ko_ref[...]], axis=0)
    grad = jnp.dot(x, k, preferred_element_type=F32)
    n, own, features = out0.shape
    held_ref[...] = (w_ref[...].astype(F32) - ETA * grad).astype(BF).reshape(held_ref.shape)
    for k, out in enumerate((out0, out1, out2, out3)):
        out[...] = held_ref[:, x_ref[0] ^ k]


def inner_step(x, xs, k_same, k_other, w, block=256):
    rows, features = w.shape
    half = k_same.shape[0]
    ny, nz, nx = SIZES[:3]
    own = rows // (ny * nz * nx)
    part = block // (nx * own)
    return call(
        inner_kernel,
        (jax.ShapeDtypeStruct((ny * nz, own, features), BF),) * nx,
        flops=4 * rows * half * features,
        moved=4 * (rows * half + w.size + k_same.size),
        grid=(rows // block,),
        in_specs=[pl.BlockSpec(memory_space=pltpu.SMEM)]
        + [pl.BlockSpec((block, v.shape[1]), lambda i: (i, 0)) for v in xs]
        + [
            pl.BlockSpec((half, features), lambda i: (0, 0)),
            pl.BlockSpec((half, features), lambda i: (0, 0)),
            pl.BlockSpec((block, features), lambda i: (i, 0)),
        ],
        out_specs=(pl.BlockSpec((part, own, features), lambda i: (i, 0, 0)),) * nx,
        scratch_shapes=[pltpu.VMEM((part, nx, own, features), BF)],
    )(x.reshape(1), *xs, k_same, k_other, w)


def x_sum_kernel(a_ref, b_ref, c_ref, d_ref, out_ref):
    total = a_ref[...].astype(F32) + b_ref[...].astype(F32)
    total += c_ref[...].astype(F32)
    total += d_ref[...].astype(F32)
    out_ref[...] = total.astype(BF)


def x_sum(shares):
    return call(x_sum_kernel, jax.ShapeDtypeStruct(shares[0].shape, BF), moved=10 * shares[0].size)(*shares)


def total_kernel(l_ref, out_ref, low_ref):
    total = l_ref[0].astype(F32)
    for i in range(1, l_ref.shape[0]):
        total += l_ref[i].astype(F32)
    out_ref[...] = total
    low_ref[...] = total.astype(BF)


def half_total(shares):
    shape = shares.shape[1:]
    return call(
        total_kernel,
        (jax.ShapeDtypeStruct(shape, F32), jax.ShapeDtypeStruct(shape, BF)),
        moved=2 * shares.size,
    )(shares)


def outer_kernel(zh_ref, s_ref, o_ref, am_ref, pam_ref, base_ref, mom_ref, all_ref):
    zh = zh_ref[0]
    own = am_ref.shape[1]
    n_rep = SIZES[0] * SIZES[1] * SIZES[2]

    def step(which, held):
        rows = pl.ds(pl.multiple_of(which * own, own), own)
        average = (s_ref[rows] + o_ref[rows].astype(F32)) / n_rep
        base = held[0]
        delta = base - average
        new_mom = MOMENT * held[1] + delta
        return rows, base - OUTER_RATE * (delta + MOMENT * new_mom), new_mom

    rows, new_base, new_mom = step(zh, am_ref)
    base_ref[0] = new_base
    mom_ref[0] = new_mom
    partner_rows, partner_base, _ = step(1 - zh, pam_ref)
    low, partner_low = new_base.astype(BF), partner_base.astype(BF)
    for i in range(all_ref.shape[0]):
        all_ref[i, rows] = low
        all_ref[i, partner_rows] = partner_low


def outer_step(zh, total, other, held, partner_held, n):
    own, features = held.shape[1:]
    vmem = pl.BlockSpec(memory_space=pltpu.VMEM)
    return call(
        outer_kernel,
        (
            jax.ShapeDtypeStruct((1, own, features), F32),
            jax.ShapeDtypeStruct((1, own, features), F32),
            jax.ShapeDtypeStruct((n, *total.shape), BF),
        ),
        moved=2 * n * total.size,
        in_specs=[pl.BlockSpec(memory_space=pltpu.SMEM)] + [vmem] * 4,
        out_specs=(vmem,) * 3,
    )(zh.reshape(1), total, other, held, partner_held)


def mix_kernel(x_ref, *refs):
    *refs, out_ref = refs
    n = len(refs) // 2
    for k in range(n):
        mixed = (1.0 - MIX_RATE) * refs[k][...].astype(F32) + MIX_RATE * refs[n + k][...].astype(F32)
        out_ref[:, x_ref[0] ^ k] = mixed.astype(BF)


def mix(x, locals_, bases, block=4):
    n, own, features = locals_[0].shape
    nx = len(locals_)
    piece = pl.BlockSpec((block, own, features), lambda i: (i, 0, 0))
    return call(
        mix_kernel,
        jax.ShapeDtypeStruct((n, nx, own, features), BF),
        moved=6 * nx * locals_[0].size,
        grid=(n // block,),
        in_specs=[pl.BlockSpec(memory_space=pltpu.SMEM)] + [piece] * (2 * nx),
        out_specs=pl.BlockSpec((block, nx, own, features), lambda i: (i, 0, 0, 0)),
    )(x.reshape(1), *locals_, *bases)


def across(value, axis, k):
    return lax.ppermute(value, axis, [(i, i ^ k) for i in range(4)])


def body(tokens, cotangent, local_weights, anchor, momentum):
    own = local_weights[0]
    depth, features = own.shape
    width = tokens.shape[1] // SIZES[3]
    core, zl, zh, x = (lax.axis_index(name) for name in ("core", "zl", "zh", "x"))
    chip_weights = lax.all_gather(own, "core", axis=0, tiled=True)
    got, rest = {}, tokens
    for k in (3, 2, 1, 0):
        chunk = lax.dynamic_slice_in_dim(rest, (zl ^ k) * width, width, 1)
        if k:
            rest, chunk = lax.optimization_barrier((rest, chunk))
        got[k] = across(chunk, "zl", k) if k else chunk
    mine, other = {}, {}
    parts = [project(got[0], chip_weights)]
    for k in (1, 2, 3):
        got[k], parts, other = lax.optimization_barrier((got[k], parts, other))
        parts.append(across(project(got[k], chip_weights), "zl", k))
        mine[k - 1], send = split(core, got[k - 1])
        other[k - 1] = lax.ppermute(send, "core", SWAP)
    parts, other = lax.optimization_barrier((parts, other))
    key_grad = norm_grad(parts, cotangent)
    got[3], key_grad = lax.optimization_barrier((got[3], key_grad))
    mine[3], send = split(core, got[3])
    other[3] = lax.ppermute(send, "core", SWAP)
    k_same = jnp.concatenate([key_grad] + [across(key_grad, "zl", k) for k in (1, 2, 3)], axis=0)
    k_other = lax.ppermute(k_same, "core", SWAP)
    xs = [mine[k] for k in range(4)] + [other[k] for k in range(4)]
    locals_ = inner_step(x, xs, k_same, k_other, own)
    held, first = lax.optimization_barrier((jnp.concatenate([anchor, momentum], axis=0), locals_[0]))
    partner_held = lax.ppermute(held, "zh", SWAP)
    shares = [first] + [across(locals_[k], "x", k) for k in (1, 2, 3)]
    shares, partner_held = lax.optimization_barrier((shares, partner_held))
    ny, nz = SIZES[:2]
    sums = x_sum(shares).reshape(ny, -1, features)
    total, low = half_total(lax.all_to_all(sums, "y", 0, 0, tiled=True))
    partner_total = lax.ppermute(low, "zh", SWAP)
    new_base, new_mom, spread = outer_step(zh, total, partner_total, held, partner_held, ny)
    base = lax.all_to_all(spread, "y", 0, 0, tiled=True).reshape(first.shape)
    bases = [base] + [across(base, "x", k) for k in (1, 2, 3)]
    return mix(x, locals_, bases).reshape(1, depth, features), new_base, new_mom


def solution(mesh):
    fine = Mesh(mesh.devices.reshape(SIZES), AXES)
    placed = (
        P((*REP, *FSDP), None),
        P((*REP, *FSDP), None),
        P(REP, FSDP, None),
        P(FSDP, REP, None),
        P(FSDP, REP, None),
    )
    return jax.shard_map(
        body,
        mesh=fine,
        in_specs=placed,
        out_specs=(P(REP, FSDP, None), P(FSDP, REP, None), P(FSDP, REP, None)),
        check_vma=False,
    )
```

```python
import functools

import jax
import jax.numpy as jnp
from jax import lax
from jax.experimental import pallas as pl
from jax.experimental.pallas import tpu as pltpu
from jax.sharding import Mesh
from jax.sharding import PartitionSpec as P

HD = 128
EPS = 1e-06
ETA = 1.0
MOMENT = 0.9
OUTER_RATE = 0.7
MIX_RATE = 0.5

AXES = ("y", "zh", "x", "zl", "core")
SIZES = (8, 2, 4, 4, 2)
REP = ("y", "zh", "x")
FSDP = ("zl", "core")
SWAP = [(0, 1), (1, 0)]
BF = jnp.bfloat16
F32 = jnp.float32
LIMIT = 16 * 1024 * 1024


def call(kernel, out_shape, flops=0, moved=0, **more):
    return pl.pallas_call(
        kernel,
        out_shape=out_shape,
        compiler_params=pltpu.CompilerParams(vmem_limit_bytes=LIMIT),
        cost_estimate=pl.CostEstimate(flops=flops, bytes_accessed=moved, transcendentals=0),
        **more,
    )


def slice_kernel(zl_ref, x_ref, *refs):
    *outs, sems = refs
    width = outs[0].shape[1]
    copies = []
    for k, out in enumerate(outs):
        start = pl.multiple_of((zl_ref[0] ^ k) * width, width)
        copies.append(pltpu.make_async_copy(x_ref.at[:, pl.ds(start, width)], out, sems.at[k]))
    for copy in copies:
        copy.start()
    for copy in copies:
        copy.wait()


def slices(zl, tokens, n):
    rows, width = tokens.shape
    return call(
        slice_kernel,
        (jax.ShapeDtypeStruct((rows, width // n), BF),) * n,
        in_specs=[pl.BlockSpec(memory_space=pltpu.SMEM), pl.BlockSpec(memory_space=pl.ANY)],
        out_specs=(pl.BlockSpec(memory_space=pltpu.VMEM),) * n,
        scratch_shapes=[pltpu.SemaphoreType.DMA((n,))],
    )(zl.reshape(1), tokens)


def project_kernel(x_ref, w_ref, out_ref):
    out_ref[...] = jnp.dot(x_ref[...], w_ref[...], preferred_element_type=F32).astype(BF)


def project(x, w):
    rows, depth = x.shape
    features = w.shape[1]
    return call(
        project_kernel,
        jax.ShapeDtypeStruct((rows, features), BF),
        flops=2 * rows * depth * features,
        moved=2 * (x.size + w.size),
    )(x, w)


def norm_kernel(a_ref, b_ref, c_ref, d_ref, g_ref, out_ref):
    for h in range(g_ref.shape[1] // HD):
        cols = pl.ds(h * HD, HD)
        projected = a_ref[:, cols].astype(F32)
        for ref in (b_ref, c_ref, d_ref):
            projected += ref[:, cols].astype(F32)
        scale = lax.rsqrt(jnp.mean(projected * projected, axis=-1, keepdims=True) + EPS)
        normed = projected * scale
        upstream = g_ref[:, cols].astype(F32)
        back = scale * (upstream - normed * jnp.mean(upstream * normed, axis=-1, keepdims=True))
        out_ref[:, cols] = back.astype(BF)


def norm_grad(parts, cotangent):
    return call(
        norm_kernel,
        jax.ShapeDtypeStruct(cotangent.shape, BF),
        moved=6 * cotangent.size * 2,
    )(*parts, cotangent)


def flip_kernel(x_ref, out_ref):
    out_ref[...] = x_ref[...].T


def flip(x):
    return call(flip_kernel, jax.ShapeDtypeStruct(x.shape[::-1], BF), moved=4 * x.size)(x)


def grad_kernel(half_ref, *refs, block):
    *refs, out_ref = refs
    xs, ks = refs[: len(refs) // 2], refs[len(refs) // 2 :]
    k = jnp.concatenate([ref[...] for ref in ks], axis=0)
    depth = out_ref.shape[0]
    for i in range(depth // block):
        start = pl.multiple_of(half_ref[0] * depth + i * block, block)
        x = jnp.concatenate([ref[pl.ds(start, block)] for ref in xs], axis=1)
        grad = jnp.dot(x, k, preferred_element_type=F32)
        out_ref[pl.ds(i * block, block)] = grad.astype(out_ref.dtype)


def gradient(half, xs, ks, dtype, block=256):
    depth, rows = xs[0].shape
    features = ks[0].shape[1]
    vmem = pl.BlockSpec(memory_space=pltpu.VMEM)
    return call(
        functools.partial(grad_kernel, block=block),
        jax.ShapeDtypeStruct((depth // 2, features), dtype),
        flops=len(xs) * depth * rows * features,
        in_specs=[pl.BlockSpec(memory_space=pltpu.SMEM)] + [vmem] * (2 * len(xs)),
        out_specs=vmem,
    )(half.reshape(1), *xs, *ks)


def inner_kernel(x_ref, s_ref, o_ref, w_ref, *outs):
    n, own, features = outs[0].shape
    nx = len(outs)
    for i in range(n):
        for d, out in enumerate(outs):
            rows = pl.ds(pl.multiple_of((i * nx + (x_ref[0] ^ d)) * own, own), own)
            grad = s_ref[rows] + o_ref[rows].astype(F32)
            out[i] = (w_ref[rows].astype(F32) - ETA * grad).astype(BF)


def inner_step(x, same, other, w):
    rows, features = w.shape
    ny, nz, nx = SIZES[:3]
    vmem = pl.BlockSpec(memory_space=pltpu.VMEM)
    return call(
        inner_kernel,
        (jax.ShapeDtypeStruct((ny * nz, rows // (ny * nz * nx), features), BF),) * nx,
        moved=8 * w.size,
        in_specs=[pl.BlockSpec(memory_space=pltpu.SMEM)] + [vmem] * 3,
        out_specs=(vmem,) * nx,
    )(x.reshape(1), same, other, w)


def x_sum_kernel(a_ref, b_ref, c_ref, d_ref, out_ref):
    total = a_ref[...].astype(F32) + b_ref[...].astype(F32)
    total += c_ref[...].astype(F32)
    total += d_ref[...].astype(F32)
    out_ref[...] = total.astype(BF)


def x_sum(shares):
    return call(x_sum_kernel, jax.ShapeDtypeStruct(shares[0].shape, BF), moved=10 * shares[0].size)(*shares)


def total_kernel(l_ref, out_ref, low_ref):
    total = l_ref[0].astype(F32)
    for i in range(1, l_ref.shape[0]):
        total += l_ref[i].astype(F32)
    out_ref[...] = total
    low_ref[...] = total.astype(BF)


def half_total(shares):
    shape = shares.shape[1:]
    return call(
        total_kernel,
        (jax.ShapeDtypeStruct(shape, F32), jax.ShapeDtypeStruct(shape, BF)),
        moved=2 * shares.size,
    )(shares)


def outer_kernel(zh_ref, s_ref, o_ref, am_ref, pam_ref, base_ref, mom_ref, all_ref):
    zh = zh_ref[0]
    own = am_ref.shape[1]
    n_rep = SIZES[0] * SIZES[1] * SIZES[2]

    def step(which, held):
        rows = pl.ds(pl.multiple_of(which * own, own), own)
        average = (s_ref[rows] + o_ref[rows].astype(F32)) / n_rep
        base = held[0]
        delta = base - average
        new_mom = MOMENT * held[1] + delta
        return rows, base - OUTER_RATE * (delta + MOMENT * new_mom), new_mom

    rows, new_base, new_mom = step(zh, am_ref)
    base_ref[0] = new_base
    mom_ref[0] = new_mom
    partner_rows, partner_base, _ = step(1 - zh, pam_ref)
    low, partner_low = new_base.astype(BF), partner_base.astype(BF)
    for i in range(all_ref.shape[0]):
        all_ref[i, rows] = low
        all_ref[i, partner_rows] = partner_low


def outer_step(zh, total, other, held, partner_held, n):
    own, features = held.shape[1:]
    vmem = pl.BlockSpec(memory_space=pltpu.VMEM)
    return call(
        outer_kernel,
        (
            jax.ShapeDtypeStruct((1, own, features), F32),
            jax.ShapeDtypeStruct((1, own, features), F32),
            jax.ShapeDtypeStruct((n, *total.shape), BF),
        ),
        moved=2 * n * total.size,
        in_specs=[pl.BlockSpec(memory_space=pltpu.SMEM)] + [vmem] * 4,
        out_specs=(vmem,) * 3,
    )(zh.reshape(1), total, other, held, partner_held)


def mix_kernel(x_ref, *refs):
    *refs, out_ref = refs
    n = len(refs) // 2
    for k in range(n):
        mixed = (1.0 - MIX_RATE) * refs[k][...].astype(F32) + MIX_RATE * refs[n + k][...].astype(F32)
        out_ref[:, x_ref[0] ^ k] = mixed.astype(BF)


def mix(x, locals_, bases, block=4):
    n, own, features = locals_[0].shape
    nx = len(locals_)
    piece = pl.BlockSpec((block, own, features), lambda i: (i, 0, 0))
    return call(
        mix_kernel,
        jax.ShapeDtypeStruct((n, nx, own, features), BF),
        moved=6 * nx * locals_[0].size,
        grid=(n // block,),
        in_specs=[pl.BlockSpec(memory_space=pltpu.SMEM)] + [piece] * (2 * nx),
        out_specs=pl.BlockSpec((block, nx, own, features), lambda i: (i, 0, 0, 0)),
    )(x.reshape(1), *locals_, *bases)


def across(value, axis, k):
    return lax.ppermute(value, axis, [(i, i ^ k) for i in range(4)])


def body(tokens, cotangent, local_weights, anchor, momentum):
    own = local_weights[0]
    depth, features = own.shape
    width = tokens.shape[1] // SIZES[3]
    core, zl, zh, x = (lax.axis_index(name) for name in ("core", "zl", "zh", "x"))
    chip_weights = lax.all_gather(own, "core", axis=0, tiled=True)
    chunks = slices(zl, tokens, SIZES[3])
    got = {k: across(chunks[k], "zl", k) for k in (3, 2, 1)}
    got[0] = chunks[0]
    held = jnp.concatenate([anchor, momentum], axis=0)
    partner_held = lax.ppermute(held, "zh", SWAP)
    parts = [project(got[0], chip_weights)]
    turned = {0: flip(got[0])}
    got[1], parts[0], turned[0] = lax.optimization_barrier((got[1], parts[0], turned[0]))
    parts.append(across(project(got[1], chip_weights), "zl", 1))
    turned[1] = flip(got[1])
    got[2], parts, turned = lax.optimization_barrier((got[2], parts, turned))
    made = project(got[2], chip_weights)
    parts.append(across(made, "zl", 2))
    got[3], made, partner_held = lax.optimization_barrier((got[3], made, partner_held))
    parts.append(across(project(got[3], chip_weights), "zl", 3))
    turned[2], turned[3] = flip(got[2]), flip(got[3])
    key_grad = norm_grad(parts, cotangent)
    ks = [key_grad] + [across(key_grad, "zl", k) for k in (1, 2, 3)]
    xs = [turned[k] for k in range(4)]
    send = gradient(1 - core, xs, ks, BF)
    same = gradient(core, xs, ks, F32)
    locals_ = inner_step(x, same, lax.ppermute(send, "core", SWAP), own)
    shares = [locals_[0]] + [across(locals_[k], "x", k) for k in (1, 2, 3)]
    ny, nz = SIZES[:2]
    sums = x_sum(shares).reshape(ny, -1, features)
    total, low = half_total(lax.all_to_all(sums, "y", 0, 0, tiled=True))
    partner_total = lax.ppermute(low, "zh", SWAP)
    new_base, new_mom, spread = outer_step(zh, total, partner_total, held, partner_held, ny)
    base = lax.all_to_all(spread, "y", 0, 0, tiled=True).reshape(locals_[0].shape)
    bases = [base] + [across(base, "x", k) for k in (1, 2, 3)]
    return mix(x, locals_, bases).reshape(1, depth, features), new_base, new_mom


def solution(mesh):
    fine = Mesh(mesh.devices.reshape(SIZES), AXES)
    placed = (
        P((*REP, *FSDP), None),
        P((*REP, *FSDP), None),
        P(REP, FSDP, None),
        P(FSDP, REP, None),
        P(FSDP, REP, None),
    )
    return jax.shard_map(
        body,
        mesh=fine,
        in_specs=placed,
        out_specs=(P(REP, FSDP, None), P(FSDP, REP, None), P(FSDP, REP, None)),
        check_vma=False,
    )
```

```python
import functools

import jax
import jax.numpy as jnp
from jax import lax
from jax.experimental import pallas as pl
from jax.experimental.pallas import tpu as pltpu
from jax.sharding import Mesh
from jax.sharding import PartitionSpec as P

HD = 128
EPS = 1e-06
ETA = 1.0
MOMENT = 0.9
OUTER_RATE = 0.7
MIX_RATE = 0.5

AXES = ("y", "zh", "x", "zl", "core")
SIZES = (8, 2, 4, 4, 2)
REP = ("y", "zh", "x")
FSDP = ("zl", "core")
N_REP = SIZES[0] * SIZES[1] * SIZES[2]
SHARE = OUTER_RATE * (1.0 + MOMENT)
SWAP = [(0, 1), (1, 0)]
BF = jnp.bfloat16
F32 = jnp.float32
LIMIT = 12 * 1024 * 1024


def call(kernel, out_shape, flops=0, moved=0, limit=LIMIT, **more):
    return pl.pallas_call(
        kernel,
        out_shape=out_shape,
        compiler_params=pltpu.CompilerParams(vmem_limit_bytes=limit),
        cost_estimate=pl.CostEstimate(flops=flops, bytes_accessed=moved, transcendentals=0),
        **more,
    )


def slice_kernel(zl_ref, x_ref, *refs):
    *outs, sems = refs
    width = outs[0].shape[1]
    copies = []
    for k, out in enumerate(outs):
        start = pl.multiple_of((zl_ref[0] ^ k) * width, width)
        copies.append(pltpu.make_async_copy(x_ref.at[:, pl.ds(start, width)], out, sems.at[k]))
    for copy in copies:
        copy.start()
    for copy in copies:
        copy.wait()


def slices(zl, tokens, n):
    rows, width = tokens.shape
    return call(
        slice_kernel,
        (pltpu.VMEM((rows, width // n), BF),) * n,
        limit=56 * 1024 * 1024,
        in_specs=[pl.BlockSpec(memory_space=pltpu.SMEM), pl.BlockSpec(memory_space=pl.ANY)],
        out_specs=(pl.BlockSpec(memory_space=pltpu.VMEM),) * n,
        scratch_shapes=[pltpu.SemaphoreType.DMA((n,))],
    )(zl.reshape(1), tokens)


def project_kernel(x_ref, w_ref, out_ref):
    out_ref[...] = jnp.dot(x_ref[...], w_ref[...], preferred_element_type=F32).astype(BF)


def project(x, w):
    rows, depth = x.shape
    features = w.shape[1]
    return call(
        project_kernel,
        jax.ShapeDtypeStruct((rows, features), BF),
        flops=2 * rows * depth * features,
        moved=2 * (x.size + w.size),
    )(x, w)


def norm_kernel(a_ref, b_ref, c_ref, d_ref, g_ref, out_ref):
    for h in range(g_ref.shape[1] // HD):
        cols = pl.ds(h * HD, HD)
        projected = a_ref[:, cols].astype(F32)
        for ref in (b_ref, c_ref, d_ref):
            projected += ref[:, cols].astype(F32)
        scale = lax.rsqrt(jnp.mean(projected * projected, axis=-1, keepdims=True) + EPS)
        normed = projected * scale
        upstream = g_ref[:, cols].astype(F32)
        back = scale * (upstream - normed * jnp.mean(upstream * normed, axis=-1, keepdims=True))
        out_ref[:, cols] = back.astype(BF)


def norm_grad(parts, cotangent):
    return call(
        norm_kernel,
        jax.ShapeDtypeStruct(cotangent.shape, BF),
        moved=6 * cotangent.size * 2,
    )(*parts, cotangent)


def flip_kernel(x_ref, out_ref):
    out_ref[...] = x_ref[...].T


def flip(x):
    return call(flip_kernel, jax.ShapeDtypeStruct(x.shape[::-1], BF), moved=4 * x.size)(x)


def grad_kernel(half_ref, *refs, block):
    *refs, out_ref = refs
    xs, ks = refs[: len(refs) // 2], refs[len(refs) // 2 :]
    k = jnp.concatenate([ref[...] for ref in ks], axis=0)
    depth = out_ref.shape[0]
    for i in range(depth // block):
        start = pl.multiple_of(half_ref[0] * depth + i * block, block)
        x = jnp.concatenate([ref[pl.ds(start, block)] for ref in xs], axis=1)
        grad = jnp.dot(x, k, preferred_element_type=F32)
        out_ref[pl.ds(i * block, block)] = grad.astype(out_ref.dtype)


def gradient(half, xs, ks, dtype, block=256):
    depth, rows = xs[0].shape
    features = ks[0].shape[1]
    vmem = pl.BlockSpec(memory_space=pltpu.VMEM)
    return call(
        functools.partial(grad_kernel, block=block),
        pltpu.VMEM((depth // 2, features), dtype),
        flops=len(xs) * depth * rows * features,
        in_specs=[pl.BlockSpec(memory_space=pltpu.SMEM)] + [vmem] * (2 * len(xs)),
        out_specs=vmem,
    )(half.reshape(1), *xs, *ks)


def inner_kernel(s_ref, o_ref, w_ref, out_ref):
    ny, nx, nz, own, _ = out_ref.shape
    for y in range(ny):
        rows = pl.ds(y * nz * nx * own, nz * nx * own)
        grad = s_ref[rows] + o_ref[rows].astype(F32)
        local = (w_ref[rows].astype(F32) - ETA * grad).astype(BF)
        for z in range(nz):
            for x in range(nx):
                start = (z * nx + x) * own
                out_ref[y, x, z] = local[start : start + own]


def inner_step(same, other, w):
    rows, features = w.shape
    ny, nz, nx = SIZES[:3]
    return call(
        inner_kernel,
        pltpu.VMEM((ny, nx, nz, rows // (ny * nz * nx), features), BF),
        moved=8 * w.size,
        in_specs=[pl.BlockSpec(memory_space=pltpu.VMEM)] * 3,
        out_specs=pl.BlockSpec(memory_space=pltpu.VMEM),
    )(same, other, w)


def total_kernel(zh_ref, l_ref, a_ref, m_ref, out_ref, low_ref):
    own = a_ref.shape[1]
    total = l_ref[0].astype(F32)
    for i in range(1, l_ref.shape[0]):
        total += l_ref[i].astype(F32)
    out_ref[...] = total
    low_ref[...] = total.astype(BF)
    rows = pl.ds(pl.multiple_of(zh_ref[0] * own, own), own)
    from_base = (1.0 - SHARE) * a_ref[0] - OUTER_RATE * MOMENT * MOMENT * m_ref[0]
    low_ref[rows] = (out_ref[rows] + from_base * (N_REP / SHARE)).astype(BF)


def half_total(zh, shares, anchor, momentum):
    shape = shares.shape[1:]
    vmem = pl.BlockSpec(memory_space=pltpu.VMEM)
    return call(
        total_kernel,
        (jax.ShapeDtypeStruct(shape, F32), jax.ShapeDtypeStruct(shape, BF)),
        moved=2 * shares.size,
        in_specs=[pl.BlockSpec(memory_space=pltpu.SMEM)] + [vmem] * 3,
        out_specs=(vmem,) * 2,
    )(zh.reshape(1), shares, anchor, momentum)


def outer_kernel(zh_ref, s_ref, o_ref, a_ref, m_ref, base_ref, mom_ref, all_ref):
    own = a_ref.shape[1]
    rows = pl.ds(pl.multiple_of(zh_ref[0] * own, own), own)
    partner_rows = pl.ds(pl.multiple_of((1 - zh_ref[0]) * own, own), own)
    average = (s_ref[rows] + o_ref[rows].astype(F32)) / N_REP
    base = a_ref[0]
    delta = base - average
    new_mom = MOMENT * m_ref[0] + delta
    new_base = base - OUTER_RATE * (delta + MOMENT * new_mom)
    mom_ref[0] = new_mom
    base_ref[0] = new_base
    low = new_base.astype(BF)
    partner_low = ((s_ref[partner_rows] + o_ref[partner_rows].astype(F32)) * (SHARE / N_REP)).astype(BF)
    for i in range(all_ref.shape[0]):
        all_ref[i, rows] = low
        all_ref[i, partner_rows] = partner_low


def outer_step(zh, total, other, anchor, momentum, n):
    vmem = pl.BlockSpec(memory_space=pltpu.VMEM)
    return call(
        outer_kernel,
        (
            jax.ShapeDtypeStruct(anchor.shape, F32),
            jax.ShapeDtypeStruct(anchor.shape, F32),
            jax.ShapeDtypeStruct((n, *total.shape), BF),
        ),
        moved=2 * n * total.size,
        in_specs=[pl.BlockSpec(memory_space=pltpu.SMEM)] + [vmem] * 4,
        out_specs=(vmem,) * 3,
    )(zh.reshape(1), total, other, anchor, momentum)


def mix_kernel(l_ref, b_ref, out_ref):
    mixed = (1.0 - MIX_RATE) * l_ref[...].astype(F32) + MIX_RATE * b_ref[...].astype(F32)
    mixed = mixed.astype(BF)
    ny, nx, nz, own, _ = l_ref.shape
    for y in range(ny):
        for z in range(nz):
            for x in range(nx):
                out_ref[0, pl.ds(((y * nz + z) * nx + x) * own, own)] = mixed[y, x, z]


def mix(local, base, block=2):
    ny, nx, nz, own, features = local.shape
    rows = nx * nz * own
    return call(
        mix_kernel,
        jax.ShapeDtypeStruct((1, ny * rows, features), BF),
        moved=6 * local.size,
        grid=(ny // block,),
        in_specs=[pl.BlockSpec((block, nx, nz, own, features), lambda i: (i, 0, 0, 0, 0))] * 2,
        out_specs=pl.BlockSpec((1, block * rows, features), lambda i: (0, i, 0)),
    )(local, base)


def across(value, axis, k):
    return lax.ppermute(value, axis, [(i, i ^ k) for i in range(4)])


def body(tokens, cotangent, local_weights, anchor, momentum):
    own = local_weights[0]
    depth, features = own.shape
    width = tokens.shape[1] // SIZES[3]
    core, zl, zh = (lax.axis_index(name) for name in ("core", "zl", "zh"))
    chip_weights = lax.all_gather(own, "core", axis=0, tiled=True)
    chunks = slices(zl, tokens, SIZES[3])
    got = {k: across(chunks[k], "zl", k) for k in (3, 2, 1)}
    got[0] = chunks[0]
    parts = [project(got[0], chip_weights)]
    turned = {0: flip(got[0])}
    got[1], parts[0], turned[0] = lax.optimization_barrier((got[1], parts[0], turned[0]))
    parts.append(across(project(got[1], chip_weights), "zl", 1))
    turned[1] = flip(got[1])
    got[2], parts, turned = lax.optimization_barrier((got[2], parts, turned))
    made = project(got[2], chip_weights)
    parts.append(across(made, "zl", 2))
    got[3], made = lax.optimization_barrier((got[3], made))
    parts.append(across(project(got[3], chip_weights), "zl", 3))
    turned[2], turned[3] = flip(got[2]), flip(got[3])
    key_grad = norm_grad(parts, cotangent)
    ks = [key_grad] + [across(key_grad, "zl", k) for k in (1, 2, 3)]
    xs = [turned[k] for k in range(4)]
    send = gradient(1 - core, xs, ks, BF)
    same = gradient(core, xs, ks, F32)
    local = inner_step(same, lax.ppermute(send, "core", SWAP), own)
    ny, nx, nz, rows, _ = local.shape
    shares = lax.all_to_all(local.reshape(ny * nx, nz * rows, features), ("y", "x"), 0, 0, tiled=True)
    total, low = half_total(zh, shares, anchor, momentum)
    partner_total = lax.ppermute(low, "zh", SWAP)
    new_base, new_mom, spread = outer_step(zh, total, partner_total, anchor, momentum, ny * nx)
    base = lax.all_to_all(spread, ("y", "x"), 0, 0, tiled=True).reshape(local.shape)
    return mix(local, base), new_base, new_mom


def solution(mesh):
    fine = Mesh(mesh.devices.reshape(SIZES), AXES)
    placed = (
        P((*REP, *FSDP), None),
        P((*REP, *FSDP), None),
        P(REP, FSDP, None),
        P(FSDP, REP, None),
        P(FSDP, REP, None),
    )
    return jax.shard_map(
        body,
        mesh=fine,
        in_specs=placed,
        out_specs=(P(REP, FSDP, None), P(FSDP, REP, None), P(FSDP, REP, None)),
        check_vma=False,
    )
```

```python
import functools

import jax
import jax.numpy as jnp
from jax import lax
from jax.experimental import pallas as pl
from jax.experimental.pallas import tpu as pltpu
from jax.sharding import Mesh
from jax.sharding import PartitionSpec as P

HD = 128
EPS = 1e-06
ETA = 1.0
MOMENT = 0.9
OUTER_RATE = 0.7
MIX_RATE = 0.5

AXES = ("y", "zh", "x", "zl", "core")
SIZES = (8, 2, 4, 4, 2)
REP = ("y", "zh", "x")
FSDP = ("zl", "core")
N_REP = SIZES[0] * SIZES[1] * SIZES[2]
SHARE = OUTER_RATE * (1.0 + MOMENT)
SWAP = [(0, 1), (1, 0)]
BF = jnp.bfloat16
F32 = jnp.float32
LIMIT = 12 * 1024 * 1024


def call(kernel, out_shape, flops=0, moved=0, limit=LIMIT, **more):
    return pl.pallas_call(
        kernel,
        out_shape=out_shape,
        compiler_params=pltpu.CompilerParams(vmem_limit_bytes=limit),
        cost_estimate=pl.CostEstimate(flops=flops, bytes_accessed=moved, transcendentals=0),
        **more,
    )


def slice_kernel(zl_ref, x_ref, *refs, distances):
    *outs, sems = refs
    width = outs[0].shape[1]
    copies = []
    for i, (k, out) in enumerate(zip(distances, outs)):
        start = pl.multiple_of((zl_ref[0] ^ k) * width, width)
        copies.append(pltpu.make_async_copy(x_ref.at[:, pl.ds(start, width)], out, sems.at[i]))
    for copy in copies:
        copy.start()
    for copy in copies:
        copy.wait()


def slices(zl, tokens, distances):
    rows, width = tokens.shape
    n = len(distances)
    return call(
        functools.partial(slice_kernel, distances=distances),
        (pltpu.VMEM((rows, width // SIZES[3]), BF),) * n,
        limit=56 * 1024 * 1024,
        in_specs=[pl.BlockSpec(memory_space=pltpu.SMEM), pl.BlockSpec(memory_space=pl.ANY)],
        out_specs=(pl.BlockSpec(memory_space=pltpu.VMEM),) * n,
        scratch_shapes=[pltpu.SemaphoreType.DMA((n,))],
    )(zl.reshape(1), tokens)


def project_kernel(core_ref, x_ref, own_ref, other_ref, out_ref):
    depth = own_ref.shape[0]
    mine = pl.ds(pl.multiple_of(core_ref[0] * depth, depth), depth)
    others = pl.ds(pl.multiple_of((1 - core_ref[0]) * depth, depth), depth)
    total = jnp.dot(x_ref[:, mine], own_ref[...], preferred_element_type=F32)
    total += jnp.dot(x_ref[:, others], other_ref[...], preferred_element_type=F32)
    out_ref[...] = total.astype(BF)


def project(core, x, own, other):
    rows, depth = x.shape
    features = own.shape[1]
    vmem = pl.BlockSpec(memory_space=pltpu.VMEM)
    return call(
        project_kernel,
        jax.ShapeDtypeStruct((rows, features), BF),
        flops=2 * rows * depth * features,
        in_specs=[pl.BlockSpec(memory_space=pltpu.SMEM)] + [vmem] * 3,
        out_specs=vmem,
    )(core.reshape(1), x, own, other)


def norm_kernel(a_ref, b_ref, c_ref, d_ref, g_ref, out_ref):
    for h in range(g_ref.shape[1] // HD):
        cols = pl.ds(h * HD, HD)
        projected = a_ref[:, cols].astype(F32)
        for ref in (b_ref, c_ref, d_ref):
            projected += ref[:, cols].astype(F32)
        scale = lax.rsqrt(jnp.mean(projected * projected, axis=-1, keepdims=True) + EPS)
        normed = projected * scale
        upstream = g_ref[:, cols].astype(F32)
        back = scale * (upstream - normed * jnp.mean(upstream * normed, axis=-1, keepdims=True))
        out_ref[:, cols] = back.astype(BF)


def norm_grad(parts, cotangent):
    return call(
        norm_kernel,
        jax.ShapeDtypeStruct(cotangent.shape, BF),
        moved=6 * cotangent.size * 2,
    )(*parts, cotangent)


def flip_kernel(x_ref, out_ref):
    out_ref[...] = x_ref[...].T


def flip(x):
    return call(flip_kernel, jax.ShapeDtypeStruct(x.shape[::-1], BF))(x)


def grad_kernel(half_ref, *refs, block):
    *refs, out_ref = refs
    xs, ks = refs[: len(refs) // 2], refs[len(refs) // 2 :]
    k = jnp.concatenate([ref[...] for ref in ks], axis=0)
    depth = out_ref.shape[0]
    for i in range(depth // block):
        start = pl.multiple_of(half_ref[0] * depth + i * block, block)
        x = jnp.concatenate([ref[pl.ds(start, block)] for ref in xs], axis=1)
        grad = jnp.dot(x, k, preferred_element_type=F32)
        out_ref[pl.ds(i * block, block)] = grad.astype(out_ref.dtype)


def gradient(half, xs, ks, dtype, block=256):
    depth, rows = xs[0].shape
    features = ks[0].shape[1]
    vmem = pl.BlockSpec(memory_space=pltpu.VMEM)
    return call(
        functools.partial(grad_kernel, block=block),
        pltpu.VMEM((depth // 2, features), dtype),
        flops=len(xs) * depth * rows * features,
        in_specs=[pl.BlockSpec(memory_space=pltpu.SMEM)] + [vmem] * (2 * len(xs)),
        out_specs=vmem,
    )(half.reshape(1), *xs, *ks)


def inner_kernel(s_ref, o_ref, w_ref, out_ref):
    ny, nx, nz, own, _ = out_ref.shape
    for y in range(ny):
        rows = pl.ds(y * nz * nx * own, nz * nx * own)
        grad = s_ref[rows] + o_ref[rows].astype(F32)
        local = (w_ref[rows].astype(F32) - ETA * grad).astype(BF)
        for z in range(nz):
            for x in range(nx):
                start = (z * nx + x) * own
                out_ref[y, x, z] = local[start : start + own]


def inner_step(same, other, w):
    rows, features = w.shape
    ny, nz, nx = SIZES[:3]
    return call(
        inner_kernel,
        pltpu.VMEM((ny, nx, nz, rows // (ny * nz * nx), features), BF),
        moved=8 * w.size,
        in_specs=[pl.BlockSpec(memory_space=pltpu.VMEM)] * 3,
        out_specs=pl.BlockSpec(memory_space=pltpu.VMEM),
    )(same, other, w)


def total_kernel(zh_ref, l_ref, a_ref, m_ref, out_ref, low_ref):
    own = a_ref.shape[1]
    total = l_ref[0].astype(F32)
    for i in range(1, l_ref.shape[0]):
        total += l_ref[i].astype(F32)
    out_ref[...] = total
    low_ref[...] = total.astype(BF)
    rows = pl.ds(pl.multiple_of(zh_ref[0] * own, own), own)
    from_base = (1.0 - SHARE) * a_ref[0] - OUTER_RATE * MOMENT * MOMENT * m_ref[0]
    low_ref[rows] = (out_ref[rows] + from_base * (N_REP / SHARE)).astype(BF)


def half_total(zh, shares, anchor, momentum):
    shape = shares.shape[1:]
    vmem = pl.BlockSpec(memory_space=pltpu.VMEM)
    return call(
        total_kernel,
        (jax.ShapeDtypeStruct(shape, F32), jax.ShapeDtypeStruct(shape, BF)),
        moved=2 * shares.size,
        in_specs=[pl.BlockSpec(memory_space=pltpu.SMEM)] + [vmem] * 3,
        out_specs=(vmem,) * 2,
    )(zh.reshape(1), shares, anchor, momentum)


def outer_kernel(zh_ref, s_ref, o_ref, a_ref, m_ref, base_ref, mom_ref, all_ref):
    own = a_ref.shape[1]
    rows = pl.ds(pl.multiple_of(zh_ref[0] * own, own), own)
    partner_rows = pl.ds(pl.multiple_of((1 - zh_ref[0]) * own, own), own)
    average = (s_ref[rows] + o_ref[rows].astype(F32)) / N_REP
    base = a_ref[0]
    delta = base - average
    new_mom = MOMENT * m_ref[0] + delta
    new_base = base - OUTER_RATE * (delta + MOMENT * new_mom)
    mom_ref[0] = new_mom
    base_ref[0] = new_base
    low = new_base.astype(BF)
    partner_low = ((s_ref[partner_rows] + o_ref[partner_rows].astype(F32)) * (SHARE / N_REP)).astype(BF)
    for i in range(all_ref.shape[0]):
        all_ref[i, rows] = low
        all_ref[i, partner_rows] = partner_low


def outer_step(zh, total, other, anchor, momentum, n):
    vmem = pl.BlockSpec(memory_space=pltpu.VMEM)
    return call(
        outer_kernel,
        (
            jax.ShapeDtypeStruct(anchor.shape, F32),
            jax.ShapeDtypeStruct(anchor.shape, F32),
            jax.ShapeDtypeStruct((n, *total.shape), BF),
        ),
        moved=2 * n * total.size,
        in_specs=[pl.BlockSpec(memory_space=pltpu.SMEM)] + [vmem] * 4,
        out_specs=(vmem,) * 3,
    )(zh.reshape(1), total, other, anchor, momentum)


def mix_kernel(l_ref, b_ref, out_ref, held_ref, sems):
    ny, nx, nz, own, _ = l_ref.shape
    rows = nz * nx * own
    copies = []
    for y in range(ny):
        mixed = (1.0 - MIX_RATE) * l_ref[y].astype(F32) + MIX_RATE * b_ref[y].astype(F32)
        mixed = mixed.astype(BF)
        for z in range(nz):
            for x in range(nx):
                held_ref[pl.ds(((y * nz + z) * nx + x) * own, own)] = mixed[x, z]
        part = pl.ds(y * rows, rows)
        copies.append(pltpu.make_async_copy(held_ref.at[part], out_ref.at[0, part], sems.at[y]))
        copies[-1].start()
    for copy in copies:
        copy.wait()


def mix(local, base):
    ny, nx, nz, own, features = local.shape
    rows = ny * nx * nz * own
    return call(
        mix_kernel,
        jax.ShapeDtypeStruct((1, rows, features), BF),
        moved=6 * local.size,
        in_specs=[pl.BlockSpec(memory_space=pltpu.VMEM)] * 2,
        out_specs=pl.BlockSpec(memory_space=pl.ANY),
        scratch_shapes=[pltpu.VMEM((rows, features), BF), pltpu.SemaphoreType.DMA((ny,))],
    )(local, base)


def across(value, axis, k):
    return lax.ppermute(value, axis, [(i, i ^ k) for i in range(4)])


def body(tokens, cotangent, local_weights, anchor, momentum):
    own = local_weights[0]
    depth, features = own.shape
    width = tokens.shape[1] // SIZES[3]
    core, zl, zh = (lax.axis_index(name) for name in ("core", "zl", "zh"))
    got = dict(enumerate(slices(zl, tokens, (0, 1, 2, 3))))
    for k in (3, 2, 1):
        got[k] = across(got[k], "zl", k)
    swapped = lax.ppermute(own, "core", SWAP)

    def partial(k):
        return project(core, got[k], own, swapped)

    turned = {0: flip(got[0])}
    parts = [partial(0)]
    got[1], parts, turned = lax.optimization_barrier((got[1], parts, turned))
    parts.append(across(partial(1), "zl", 1))
    turned[1] = flip(got[1])
    got[2], parts, turned = lax.optimization_barrier((got[2], parts, turned))
    made = partial(2)
    parts.append(across(made, "zl", 2))
    got[3], made = lax.optimization_barrier((got[3], made))
    parts.append(across(partial(3), "zl", 3))
    key_grad = norm_grad(parts, cotangent)
    ks = [key_grad] + [across(key_grad, "zl", k) for k in (1, 2, 3)]
    for k, near in ((3, 1), (2, 2)):
        got[k], ks[near] = lax.optimization_barrier((got[k], ks[near]))
        turned[k] = flip(got[k])
    xs = [turned[k] for k in range(4)]
    xs = [turned[k] for k in range(4)]
    send = gradient(1 - core, xs, ks, BF)
    same = gradient(core, xs, ks, F32)
    local = inner_step(same, lax.ppermute(send, "core", SWAP), own)
    ny, nx, nz, rows, _ = local.shape
    shares = lax.all_to_all(local.reshape(ny * nx, nz * rows, features), ("y", "x"), 0, 0, tiled=True)
    total, low = half_total(zh, shares, anchor, momentum)
    partner_total = lax.ppermute(low, "zh", SWAP)
    new_base, new_mom, spread = outer_step(zh, total, partner_total, anchor, momentum, ny * nx)
    base = lax.all_to_all(spread, ("y", "x"), 0, 0, tiled=True).reshape(local.shape)
    return mix(local, base), new_base, new_mom


def solution(mesh):
    fine = Mesh(mesh.devices.reshape(SIZES), AXES)
    placed = (
        P((*REP, *FSDP), None),
        P((*REP, *FSDP), None),
        P(REP, FSDP, None),
        P(FSDP, REP, None),
        P(FSDP, REP, None),
    )
    return jax.shard_map(
        body,
        mesh=fine,
        in_specs=placed,
        out_specs=(P(REP, FSDP, None), P(FSDP, REP, None), P(FSDP, REP, None)),
        check_vma=False,
    )
```

```python
import functools

import jax
import jax.numpy as jnp
from jax import lax
from jax.experimental import pallas as pl
from jax.experimental.pallas import tpu as pltpu
from jax.sharding import Mesh
from jax.sharding import PartitionSpec as P

HD = 128
EPS = 1e-06
ETA = 1.0
MOMENT = 0.9
OUTER_RATE = 0.7
MIX_RATE = 0.5

AXES = ("y", "zh", "x", "zl", "core")
SIZES = (8, 2, 4, 4, 2)
REP = ("y", "zh", "x")
FSDP = ("zl", "core")
N_REP = SIZES[0] * SIZES[1] * SIZES[2]
SHARE = OUTER_RATE * (1.0 + MOMENT)
SWAP = [(0, 1), (1, 0)]
BF = jnp.bfloat16
F32 = jnp.float32
LIMIT = 12 * 1024 * 1024


def call(kernel, out_shape, flops=0, moved=0, limit=LIMIT, **more):
    return pl.pallas_call(
        kernel,
        out_shape=out_shape,
        compiler_params=pltpu.CompilerParams(vmem_limit_bytes=limit),
        cost_estimate=pl.CostEstimate(flops=flops, bytes_accessed=moved, transcendentals=0),
        **more,
    )


def slice_kernel(zl_ref, x_ref, *refs, distances):
    *outs, sems = refs
    width = outs[0].shape[1]
    copies = []
    for i, (k, out) in enumerate(zip(distances, outs)):
        start = pl.multiple_of((zl_ref[0] ^ k) * width, width)
        copies.append(pltpu.make_async_copy(x_ref.at[:, pl.ds(start, width)], out, sems.at[i]))
    for copy in copies:
        copy.start()
    for copy in copies:
        copy.wait()


def slices(zl, tokens, distances):
    rows, width = tokens.shape
    n, width = len(distances), width // SIZES[3]
    return call(
        functools.partial(slice_kernel, distances=distances),
        (pltpu.VMEM((rows, width), BF),) * n,
        in_specs=[pl.BlockSpec(memory_space=pltpu.SMEM), pl.BlockSpec(memory_space=pl.ANY)],
        out_specs=(pl.BlockSpec(memory_space=pltpu.VMEM),) * n,
        scratch_shapes=[pltpu.SemaphoreType.DMA((n,))],
    )(zl.reshape(1), tokens)


def project_kernel(core_ref, own_ref, other_ref, x_ref, out_ref):
    depth = own_ref.shape[0]
    mine = pl.ds(pl.multiple_of(core_ref[0] * depth, depth), depth)
    others = pl.ds(pl.multiple_of((1 - core_ref[0]) * depth, depth), depth)
    total = jnp.dot(x_ref[:, mine], own_ref[...], preferred_element_type=F32)
    total += jnp.dot(x_ref[:, others], other_ref[...], preferred_element_type=F32)
    out_ref[...] = total.astype(BF)


def project(core, x, own, other):
    vmem = pl.BlockSpec(memory_space=pltpu.VMEM)
    return call(
        project_kernel,
        jax.ShapeDtypeStruct((x.shape[0], own.shape[1]), BF),
        in_specs=[pl.BlockSpec(memory_space=pltpu.SMEM)] + [vmem] * 3,
        out_specs=vmem,
    )(core.reshape(1), own, other, x)


def norm_kernel(a_ref, b_ref, c_ref, d_ref, g_ref, out_ref):
    for h in range(g_ref.shape[1] // HD):
        cols = pl.ds(h * HD, HD)
        projected = a_ref[:, cols].astype(F32)
        for ref in (b_ref, c_ref, d_ref):
            projected += ref[:, cols].astype(F32)
        scale = lax.rsqrt(jnp.mean(projected * projected, axis=-1, keepdims=True) + EPS)
        normed = projected * scale
        upstream = g_ref[:, cols].astype(F32)
        back = scale * (upstream - normed * jnp.mean(upstream * normed, axis=-1, keepdims=True))
        out_ref[:, cols] = back.astype(BF)


def norm_grad(parts, cotangent):
    return call(
        norm_kernel,
        jax.ShapeDtypeStruct(cotangent.shape, BF),
        moved=6 * cotangent.size * 2,
    )(*parts, cotangent)


def flip_kernel(x_ref, out_ref):
    out_ref[...] = x_ref[...].T


def flip(x):
    return call(flip_kernel, jax.ShapeDtypeStruct(x.shape[::-1], BF))(x)


def grad_kernel(half_ref, zl_ref, *refs, block):
    *xs, k_ref, out_ref = refs
    rows = xs[0].shape[1]
    starts = [pl.multiple_of((zl_ref[0] ^ k) * rows, rows) for k in range(len(xs))]
    k = jnp.concatenate([k_ref[pl.ds(start, rows)] for start in starts], axis=0)
    depth = out_ref.shape[0]
    for i in range(depth // block):
        start = pl.multiple_of(half_ref[0] * depth + i * block, block)
        x = jnp.concatenate([ref[pl.ds(start, block)] for ref in xs], axis=1)
        grad = jnp.dot(x, k, preferred_element_type=F32)
        out_ref[pl.ds(i * block, block)] = grad.astype(out_ref.dtype)


def gradient(half, zl, xs, key_grads, dtype, block=256):
    depth, rows = xs[0].shape
    features = key_grads.shape[1]
    smem, vmem = (pl.BlockSpec(memory_space=space) for space in (pltpu.SMEM, pltpu.VMEM))
    return call(
        functools.partial(grad_kernel, block=block),
        pltpu.VMEM((depth // 2, features), dtype),
        flops=len(xs) * depth * rows * features,
        in_specs=[smem, smem] + [vmem] * (len(xs) + 1),
        out_specs=vmem,
    )(half.reshape(1), zl.reshape(1), *xs, key_grads)


def inner_kernel(s_ref, o_ref, w_ref, out_ref):
    ny, nx, nz, own, _ = out_ref.shape
    for y in range(ny):
        rows = pl.ds(y * nz * nx * own, nz * nx * own)
        grad = s_ref[rows] + o_ref[rows].astype(F32)
        local = (w_ref[rows].astype(F32) - ETA * grad).astype(BF)
        for z in range(nz):
            for x in range(nx):
                start = (z * nx + x) * own
                out_ref[y, x, z] = local[start : start + own]


def inner_step(same, other, w):
    rows, features = w.shape
    ny, nz, nx = SIZES[:3]
    return call(
        inner_kernel,
        pltpu.VMEM((ny, nx, nz, rows // (ny * nz * nx), features), BF),
        moved=8 * w.size,
        in_specs=[pl.BlockSpec(memory_space=pltpu.VMEM)] * 3,
        out_specs=pl.BlockSpec(memory_space=pltpu.VMEM),
    )(same, other, w)


def total_kernel(zh_ref, l_ref, held_ref, out_ref, low_ref):
    own = held_ref.shape[2]
    total = l_ref[0].astype(F32)
    for i in range(1, l_ref.shape[0]):
        total += l_ref[i].astype(F32)
    out_ref[...] = total
    low_ref[...] = total.astype(BF)
    rows = pl.ds(pl.multiple_of(zh_ref[0] * own, own), own)
    from_base = (1.0 - SHARE) * held_ref[0, 0] - OUTER_RATE * MOMENT * MOMENT * held_ref[1, 0]
    low_ref[rows] = (out_ref[rows] + from_base * (N_REP / SHARE)).astype(BF)


def half_total(zh, shares, held):
    shape = shares.shape[1:]
    smem, vmem = (pl.BlockSpec(memory_space=space) for space in (pltpu.SMEM, pltpu.VMEM))
    return call(
        total_kernel,
        (jax.ShapeDtypeStruct(shape, F32), jax.ShapeDtypeStruct(shape, BF)),
        in_specs=[smem, vmem, vmem],
        out_specs=(vmem,) * 2,
    )(zh.reshape(1), shares, held)


def outer_kernel(zh_ref, s_ref, o_ref, held_ref, base_ref, mom_ref, all_ref):
    own = held_ref.shape[2]
    rows = pl.ds(pl.multiple_of(zh_ref[0] * own, own), own)
    partner_rows = pl.ds(pl.multiple_of((1 - zh_ref[0]) * own, own), own)
    average = (s_ref[rows] + o_ref[rows].astype(F32)) / N_REP
    base = held_ref[0, 0]
    delta = base - average
    new_mom = MOMENT * held_ref[1, 0] + delta
    new_base = base - OUTER_RATE * (delta + MOMENT * new_mom)
    mom_ref[0] = new_mom
    base_ref[0] = new_base
    low = new_base.astype(BF)
    partner_low = ((s_ref[partner_rows] + o_ref[partner_rows].astype(F32)) * (SHARE / N_REP)).astype(BF)
    for i in range(all_ref.shape[0]):
        all_ref[i, rows] = low
        all_ref[i, partner_rows] = partner_low


def outer_step(zh, total, other, held, n):
    smem, vmem = (pl.BlockSpec(memory_space=space) for space in (pltpu.SMEM, pltpu.VMEM))
    shape = jax.ShapeDtypeStruct(held.shape[1:], F32)
    return call(
        outer_kernel,
        (shape, shape, jax.ShapeDtypeStruct((n, *total.shape), BF)),
        in_specs=[smem] + [vmem] * 3,
        out_specs=(vmem,) * 3,
    )(zh.reshape(1), total, other, held)


def hold_kernel(a_ref, m_ref, out_ref):
    out_ref[0] = a_ref[...]
    out_ref[1] = m_ref[...]


def hold(anchor, momentum):
    return call(hold_kernel, pltpu.VMEM((2, *anchor.shape), F32))(anchor, momentum)


def mix_kernel(l_ref, b_ref, out_ref, held_ref, sems):
    ny, nx, nz, own, _ = l_ref.shape
    rows = nz * nx * own
    copies = []
    for y in range(ny):
        mixed = (1.0 - MIX_RATE) * l_ref[y].astype(F32) + MIX_RATE * b_ref[y].astype(F32)
        mixed = mixed.astype(BF)
        for z in range(nz):
            for x in range(nx):
                held_ref[pl.ds(((y * nz + z) * nx + x) * own, own)] = mixed[x, z]
        part = pl.ds(y * rows, rows)
        copies.append(pltpu.make_async_copy(held_ref.at[part], out_ref.at[0, part], sems.at[y]))
        copies[-1].start()
    for copy in copies:
        copy.wait()


def mix(local, base):
    ny, nx, nz, own, features = local.shape
    rows = ny * nx * nz * own
    return call(
        mix_kernel,
        jax.ShapeDtypeStruct((1, rows, features), BF),
        moved=6 * local.size,
        in_specs=[pl.BlockSpec(memory_space=pltpu.VMEM)] * 2,
        out_specs=pl.BlockSpec(memory_space=pl.ANY),
        scratch_shapes=[pltpu.VMEM((rows, features), BF), pltpu.SemaphoreType.DMA((ny,))],
    )(local, base)


def across(value, axis, k):
    return lax.ppermute(value, axis, [(i, i ^ k) for i in range(4)])


def body(tokens, cotangent, local_weights, anchor, momentum):
    own = local_weights[0]
    depth, features = own.shape
    width = tokens.shape[1] // SIZES[3]
    core, zl, zh = (lax.axis_index(name) for name in ("core", "zl", "zh"))
    got = [None] + [across(x, "zl", k) for k, x in zip((1, 2, 3), slices(zl, tokens, (1, 2, 3)))]
    swapped = lax.ppermute(own, "core", SWAP)
    held = hold(anchor, momentum)
    (got[0],) = slices(zl, tokens, (0,))
    got[0], held = lax.optimization_barrier((got[0], held))
    parts = [project(core, got[0], own, swapped)]
    turned = [flip(got[0])]
    got[2], got[1], parts, turned = lax.optimization_barrier((got[2], got[1], parts, turned))
    made = project(core, got[1], own, swapped)
    parts.append(across(made, "zl", 1))
    for k in (2, 3):
        got[k], made = lax.optimization_barrier((got[k], made))
        made = project(core, got[k], own, swapped)
        parts.append(across(made, "zl", k))
    got, made = lax.optimization_barrier((got, made))
    turned += [flip(x) for x in got[1:]]
    parts, turned = lax.optimization_barrier((parts, turned))
    key_grad = norm_grad(parts, cotangent)
    key_grads = lax.all_gather(key_grad, "zl", axis=0, tiled=True)
    send = gradient(1 - core, zl, turned, key_grads, BF)
    same = gradient(core, zl, turned, key_grads, F32)
    local = inner_step(same, lax.ppermute(send, "core", SWAP), own)
    ny, nx, nz, rows, _ = local.shape
    shares = lax.all_to_all(local.reshape(ny * nx, nz * rows, features), ("y", "x"), 0, 0, tiled=True)
    total, low = half_total(zh, shares, held)
    partner_total = lax.ppermute(low, "zh", SWAP)
    new_base, new_mom, spread = outer_step(zh, total, partner_total, held, ny * nx)
    base = lax.all_to_all(spread, ("y", "x"), 0, 0, tiled=True).reshape(local.shape)
    return mix(local, base), new_base, new_mom


def solution(mesh):
    fine = Mesh(mesh.devices.reshape(SIZES), AXES)
    placed = (
        P((*REP, *FSDP), None),
        P((*REP, *FSDP), None),
        P(REP, FSDP, None),
        P(FSDP, REP, None),
        P(FSDP, REP, None),
    )
    return jax.shard_map(
        body,
        mesh=fine,
        in_specs=placed,
        out_specs=(P(REP, FSDP, None), P(FSDP, REP, None), P(FSDP, REP, None)),
        check_vma=False,
    )
```

```python
import functools

import jax
import jax.numpy as jnp
from jax import lax
from jax.experimental import pallas as pl
from jax.experimental.pallas import tpu as pltpu
from jax.sharding import Mesh
from jax.sharding import PartitionSpec as P

HD = 128
EPS = 1e-06
ETA = 1.0
MOMENT = 0.9
OUTER_RATE = 0.7
MIX_RATE = 0.5

AXES = ("y", "zh", "x", "zl", "core")
SIZES = (8, 2, 4, 4, 2)
REP = ("y", "zh", "x")
FSDP = ("zl", "core")
N_REP = SIZES[0] * SIZES[1] * SIZES[2]
SHARE = OUTER_RATE * (1.0 + MOMENT)
SWAP = [(0, 1), (1, 0)]
BF = jnp.bfloat16
F32 = jnp.float32
LIMIT = 12 * 1024 * 1024


def call(kernel, out_shape, flops=0, moved=0, limit=LIMIT, **more):
    return pl.pallas_call(
        kernel,
        out_shape=out_shape,
        compiler_params=pltpu.CompilerParams(vmem_limit_bytes=limit),
        cost_estimate=pl.CostEstimate(flops=flops, bytes_accessed=moved, transcendentals=0),
        **more,
    )


def slice_kernel(zl_ref, x_ref, *refs, distances):
    *outs, sems = refs
    width = outs[0].shape[1]
    copies = []
    for i, (k, out) in enumerate(zip(distances, outs)):
        start = pl.multiple_of((zl_ref[0] ^ k) * width, width)
        copies.append(pltpu.make_async_copy(x_ref.at[:, pl.ds(start, width)], out, sems.at[i]))
    for copy in copies:
        copy.start()
    for copy in copies:
        copy.wait()


def slices(zl, tokens, distances):
    rows, width = tokens.shape
    n, width = len(distances), width // SIZES[3]
    return call(
        functools.partial(slice_kernel, distances=distances),
        (pltpu.VMEM((rows, width), BF),) * n,
        in_specs=[pl.BlockSpec(memory_space=pltpu.SMEM), pl.BlockSpec(memory_space=pl.ANY)],
        out_specs=(pl.BlockSpec(memory_space=pltpu.VMEM),) * n,
        scratch_shapes=[pltpu.SemaphoreType.DMA((n,))],
    )(zl.reshape(1), tokens)


def project_kernel(core_ref, own_ref, other_ref, x_ref, out_ref):
    depth = own_ref.shape[0]
    mine = pl.ds(pl.multiple_of(core_ref[0] * depth, depth), depth)
    others = pl.ds(pl.multiple_of((1 - core_ref[0]) * depth, depth), depth)
    total = jnp.dot(x_ref[:, mine], own_ref[...], preferred_element_type=F32)
    total += jnp.dot(x_ref[:, others], other_ref[...], preferred_element_type=F32)
    out_ref[...] = total.astype(BF)


def project(core, x, own, other):
    vmem = pl.BlockSpec(memory_space=pltpu.VMEM)
    return call(
        project_kernel,
        jax.ShapeDtypeStruct((x.shape[0], own.shape[1]), BF),
        in_specs=[pl.BlockSpec(memory_space=pltpu.SMEM)] + [vmem] * 3,
        out_specs=vmem,
    )(core.reshape(1), own, other, x)


def norm_kernel(a_ref, b_ref, c_ref, d_ref, g_ref, out_ref):
    for h in range(g_ref.shape[1] // HD):
        cols = pl.ds(h * HD, HD)
        projected = a_ref[:, cols].astype(F32)
        for ref in (b_ref, c_ref, d_ref):
            projected += ref[:, cols].astype(F32)
        scale = lax.rsqrt(jnp.mean(projected * projected, axis=-1, keepdims=True) + EPS)
        normed = projected * scale
        upstream = g_ref[:, cols].astype(F32)
        back = scale * (upstream - normed * jnp.mean(upstream * normed, axis=-1, keepdims=True))
        out_ref[:, cols] = back.astype(BF)


def norm_grad(parts, cotangent):
    return call(
        norm_kernel,
        jax.ShapeDtypeStruct(cotangent.shape, BF),
        moved=6 * cotangent.size * 2,
    )(*parts, cotangent)


def flip_kernel(x_ref, out_ref):
    out_ref[...] = x_ref[...].T


def flip(x):
    return call(flip_kernel, jax.ShapeDtypeStruct(x.shape[::-1], BF))(x)


def grad_kernel(half_ref, zl_ref, *refs, block):
    *xs, k_ref, out_ref = refs
    rows = xs[0].shape[1]
    starts = [pl.multiple_of((zl_ref[0] ^ k) * rows, rows) for k in range(len(xs))]
    k = jnp.concatenate([k_ref[pl.ds(start, rows)] for start in starts], axis=0)
    depth = out_ref.shape[0]
    for i in range(depth // block):
        start = pl.multiple_of(half_ref[0] * depth + i * block, block)
        x = jnp.concatenate([ref[pl.ds(start, block)] for ref in xs], axis=1)
        grad = jnp.dot(x, k, preferred_element_type=F32)
        out_ref[pl.ds(i * block, block)] = grad.astype(out_ref.dtype)


def gradient(half, zl, xs, key_grads, dtype, block=256):
    depth, rows = xs[0].shape
    features = key_grads.shape[1]
    smem, vmem = (pl.BlockSpec(memory_space=space) for space in (pltpu.SMEM, pltpu.VMEM))
    return call(
        functools.partial(grad_kernel, block=block),
        pltpu.VMEM((depth // 2, features), dtype),
        flops=len(xs) * depth * rows * features,
        in_specs=[smem, smem] + [vmem] * (len(xs) + 1),
        out_specs=vmem,
    )(half.reshape(1), zl.reshape(1), *xs, key_grads)


def inner_kernel(s_ref, o_ref, w_ref, out_ref):
    ny, nx, nz, own, _ = out_ref.shape
    for y in range(ny):
        rows = pl.ds(y * nz * nx * own, nz * nx * own)
        grad = s_ref[rows] + o_ref[rows].astype(F32)
        local = (w_ref[rows].astype(F32) - ETA * grad).astype(BF)
        for z in range(nz):
            for x in range(nx):
                start = (z * nx + x) * own
                out_ref[y, x, z] = local[start : start + own]


def inner_step(same, other, w):
    rows, features = w.shape
    ny, nz, nx = SIZES[:3]
    return call(
        inner_kernel,
        pltpu.VMEM((ny, nx, nz, rows // (ny * nz * nx), features), BF),
        moved=8 * w.size,
        in_specs=[pl.BlockSpec(memory_space=pltpu.VMEM)] * 3,
        out_specs=pl.BlockSpec(memory_space=pltpu.VMEM),
    )(same, other, w)


def total_kernel(zh_ref, l_ref, held_ref, out_ref, low_ref):
    own = held_ref.shape[2]
    total = l_ref[0].astype(F32)
    for i in range(1, l_ref.shape[0]):
        total += l_ref[i].astype(F32)
    out_ref[...] = total
    low_ref[...] = total.astype(BF)
    rows = pl.ds(pl.multiple_of(zh_ref[0] * own, own), own)
    from_base = (1.0 - SHARE) * held_ref[0, 0] - OUTER_RATE * MOMENT * MOMENT * held_ref[1, 0]
    low_ref[rows] = (out_ref[rows] + from_base * (N_REP / SHARE)).astype(BF)


def half_total(zh, shares, held):
    shape = shares.shape[1:]
    smem, vmem = (pl.BlockSpec(memory_space=space) for space in (pltpu.SMEM, pltpu.VMEM))
    return call(
        total_kernel,
        (jax.ShapeDtypeStruct(shape, F32), jax.ShapeDtypeStruct(shape, BF)),
        in_specs=[smem, vmem, vmem],
        out_specs=(vmem,) * 2,
    )(zh.reshape(1), shares, held)


def outer_kernel(zh_ref, s_ref, o_ref, held_ref, base_ref, mom_ref, all_ref):
    own = held_ref.shape[2]
    rows = pl.ds(pl.multiple_of(zh_ref[0] * own, own), own)
    partner_rows = pl.ds(pl.multiple_of((1 - zh_ref[0]) * own, own), own)
    partner = 1 - zh_ref[0]
    average = (s_ref[rows] + o_ref[partner, rows].astype(F32)) / N_REP
    base = held_ref[0, 0]
    delta = base - average
    new_mom = MOMENT * held_ref[1, 0] + delta
    new_base = base - OUTER_RATE * (delta + MOMENT * new_mom)
    mom_ref[0] = new_mom
    base_ref[0] = new_base
    low = new_base.astype(BF)
    partner_low = ((s_ref[partner_rows] + o_ref[partner, partner_rows].astype(F32)) * (SHARE / N_REP)).astype(BF)
    for i in range(all_ref.shape[0]):
        all_ref[i, rows] = low
        all_ref[i, partner_rows] = partner_low


def outer_step(zh, total, other, held, n):
    smem, vmem = (pl.BlockSpec(memory_space=space) for space in (pltpu.SMEM, pltpu.VMEM))
    shape = jax.ShapeDtypeStruct(held.shape[1:], F32)
    return call(
        outer_kernel,
        (shape, shape, jax.ShapeDtypeStruct((n, *total.shape), BF)),
        in_specs=[smem] + [vmem] * 3,
        out_specs=(vmem,) * 3,
    )(zh.reshape(1), total, other, held)


def hold_kernel(a_ref, m_ref, out_ref):
    out_ref[0] = a_ref[...]
    out_ref[1] = m_ref[...]


def hold(anchor, momentum):
    return call(hold_kernel, pltpu.VMEM((2, *anchor.shape), F32))(anchor, momentum)


def mix_kernel(l_ref, b_ref, out_ref, held_ref, sems):
    ny, nx, nz, own, _ = l_ref.shape
    rows = nz * nx * own
    copies = []
    for y in range(ny):
        mixed = (1.0 - MIX_RATE) * l_ref[y].astype(F32) + MIX_RATE * b_ref[y].astype(F32)
        mixed = mixed.astype(BF)
        for z in range(nz):
            for x in range(nx):
                held_ref[pl.ds(((y * nz + z) * nx + x) * own, own)] = mixed[x, z]
        part = pl.ds(y * rows, rows)
        copies.append(pltpu.make_async_copy(held_ref.at[part], out_ref.at[0, part], sems.at[y]))
        copies[-1].start()
    for copy in copies:
        copy.wait()


def mix(local, base):
    ny, nx, nz, own, features = local.shape
    rows = ny * nx * nz * own
    return call(
        mix_kernel,
        jax.ShapeDtypeStruct((1, rows, features), BF),
        moved=6 * local.size,
        in_specs=[pl.BlockSpec(memory_space=pltpu.VMEM)] * 2,
        out_specs=pl.BlockSpec(memory_space=pl.ANY),
        scratch_shapes=[pltpu.VMEM((rows, features), BF), pltpu.SemaphoreType.DMA((ny,))],
    )(local, base)


def across(value, axis, k):
    return lax.ppermute(value, axis, [(i, i ^ k) for i in range(4)])


def body(tokens, cotangent, local_weights, anchor, momentum):
    own = local_weights[0]
    depth, features = own.shape
    width = tokens.shape[1] // SIZES[3]
    core, zl, zh = (lax.axis_index(name) for name in ("core", "zl", "zh"))
    got = [None] + [across(x, "zl", k) for k, x in zip((1, 2, 3), slices(zl, tokens, (1, 2, 3)))]
    swapped = lax.ppermute(own, "core", SWAP)
    held = hold(anchor, momentum)
    (got[0],) = slices(zl, tokens, (0,))
    got[0], held = lax.optimization_barrier((got[0], held))
    parts = [project(core, got[0], own, swapped)]
    turned = [flip(got[0])]
    got[2], got[1], parts, turned = lax.optimization_barrier((got[2], got[1], parts, turned))
    for k, before in ((2, None), (1, 2), (3, 1)):
        if before:
            got[k], made = lax.optimization_barrier((got[k], made))
        made = project(core, got[k], own, swapped)
        parts.append(across(made, "zl", k))
    parts[1], parts[2] = parts[2], parts[1]
    got, made = lax.optimization_barrier((got, made))
    turned += [flip(x) for x in got[1:]]
    parts, turned = lax.optimization_barrier((parts, turned))
    key_grad = norm_grad(parts, cotangent)
    key_grads = lax.all_gather(key_grad, "zl", axis=0, tiled=True)
    send = gradient(1 - core, zl, turned, key_grads, BF)
    same = gradient(core, zl, turned, key_grads, F32)
    local = inner_step(same, lax.ppermute(send, "core", SWAP), own)
    ny, nx, nz, rows, _ = local.shape
    shares = lax.all_to_all(local.reshape(ny * nx, nz * rows, features), ("y", "x"), 0, 0, tiled=True)
    total, low = half_total(zh, shares, held)
    both = lax.all_gather(low, "zh")
    new_base, new_mom, spread = outer_step(zh, total, both, held, ny * nx)
    base = lax.all_to_all(spread, ("y", "x"), 0, 0, tiled=True).reshape(local.shape)
    return mix(local, base), new_base, new_mom


def solution(mesh):
    fine = Mesh(mesh.devices.reshape(SIZES), AXES)
    placed = (
        P((*REP, *FSDP), None),
        P((*REP, *FSDP), None),
        P(REP, FSDP, None),
        P(FSDP, REP, None),
        P(FSDP, REP, None),
    )
    return jax.shard_map(
        body,
        mesh=fine,
        in_specs=placed,
        out_specs=(P(REP, FSDP, None), P(FSDP, REP, None), P(FSDP, REP, None)),
        check_vma=False,
    )
```

```python
import functools

import jax
import jax.numpy as jnp
from jax import lax
from jax.experimental import pallas as pl
from jax.experimental.pallas import tpu as pltpu
from jax.sharding import Mesh
from jax.sharding import PartitionSpec as P

HD = 128
EPS = 1e-06
ETA = 1.0
MOMENT = 0.9
OUTER_RATE = 0.7
MIX_RATE = 0.5

AXES = ("y", "zh", "x", "zl", "core")
SIZES = (8, 2, 4, 4, 2)
REP = ("y", "zh", "x")
FSDP = ("zl", "core")
N_REP = SIZES[0] * SIZES[1] * SIZES[2]
SHARE = OUTER_RATE * (1.0 + MOMENT)
SWAP = [(0, 1), (1, 0)]
BF = jnp.bfloat16
F32 = jnp.float32
LIMIT = 12 * 1024 * 1024


def call(kernel, out_shape, flops=0, moved=0, limit=LIMIT, **more):
    return pl.pallas_call(
        kernel,
        out_shape=out_shape,
        compiler_params=pltpu.CompilerParams(vmem_limit_bytes=limit),
        cost_estimate=pl.CostEstimate(flops=flops, bytes_accessed=moved, transcendentals=0),
        **more,
    )


def slice_kernel(zl_ref, x_ref, *refs, distances):
    *outs, sems = refs
    width = outs[0].shape[1]
    copies = []
    for i, (k, out) in enumerate(zip(distances, outs)):
        start = pl.multiple_of((zl_ref[0] ^ k) * width, width)
        copies.append(pltpu.make_async_copy(x_ref.at[:, pl.ds(start, width)], out, sems.at[i]))
    for copy in copies:
        copy.start()
    for copy in copies:
        copy.wait()


def slices(zl, tokens, distances):
    rows, width = tokens.shape
    n, width = len(distances), width // SIZES[3]
    return call(
        functools.partial(slice_kernel, distances=distances),
        (pltpu.VMEM((rows, width), BF),) * n,
        in_specs=[pl.BlockSpec(memory_space=pltpu.SMEM), pl.BlockSpec(memory_space=pl.ANY)],
        out_specs=(pl.BlockSpec(memory_space=pltpu.VMEM),) * n,
        scratch_shapes=[pltpu.SemaphoreType.DMA((n,))],
    )(zl.reshape(1), tokens)


def project_kernel(core_ref, own_ref, other_ref, x_ref, out_ref):
    depth = own_ref.shape[0]
    mine = pl.ds(pl.multiple_of(core_ref[0] * depth, depth), depth)
    others = pl.ds(pl.multiple_of((1 - core_ref[0]) * depth, depth), depth)
    total = jnp.dot(x_ref[:, mine], own_ref[...], preferred_element_type=F32)
    total += jnp.dot(x_ref[:, others], other_ref[...], preferred_element_type=F32)
    out_ref[...] = total.astype(BF)


def project(core, x, own, other):
    vmem = pl.BlockSpec(memory_space=pltpu.VMEM)
    return call(
        project_kernel,
        jax.ShapeDtypeStruct((x.shape[0], own.shape[1]), BF),
        in_specs=[pl.BlockSpec(memory_space=pltpu.SMEM)] + [vmem] * 3,
        out_specs=vmem,
    )(core.reshape(1), own, other, x)


def norm_kernel(a_ref, b_ref, c_ref, d_ref, g_ref, out_ref):
    for h in range(g_ref.shape[1] // HD):
        cols = pl.ds(h * HD, HD)
        projected = a_ref[:, cols].astype(F32)
        for ref in (b_ref, c_ref, d_ref):
            projected += ref[:, cols].astype(F32)
        scale = lax.rsqrt(jnp.mean(projected * projected, axis=-1, keepdims=True) + EPS)
        normed = projected * scale
        upstream = g_ref[:, cols].astype(F32)
        back = scale * (upstream - normed * jnp.mean(upstream * normed, axis=-1, keepdims=True))
        out_ref[:, cols] = back.astype(BF)


def norm_grad(parts, cotangent):
    return call(
        norm_kernel,
        jax.ShapeDtypeStruct(cotangent.shape, BF),
        moved=6 * cotangent.size * 2,
    )(*parts, cotangent)


def flip_kernel(x_ref, out_ref):
    out_ref[...] = x_ref[...].T


def flip(x):
    return call(flip_kernel, jax.ShapeDtypeStruct(x.shape[::-1], BF))(x)


def grad_kernel(half_ref, zl_ref, *refs, block):
    *xs, k_ref, out_ref = refs
    rows = xs[0].shape[1]
    starts = [pl.multiple_of((zl_ref[0] ^ k) * rows, rows) for k in range(len(xs))]
    k = jnp.concatenate([k_ref[pl.ds(start, rows)] for start in starts], axis=0)
    depth = out_ref.shape[0]
    for i in range(depth // block):
        start = pl.multiple_of(half_ref[0] * depth + i * block, block)
        x = jnp.concatenate([ref[pl.ds(start, block)] for ref in xs], axis=1)
        grad = jnp.dot(x, k, preferred_element_type=F32)
        out_ref[pl.ds(i * block, block)] = grad.astype(out_ref.dtype)


def gradient(half, zl, xs, key_grads, dtype, block=256):
    depth, rows = xs[0].shape
    features = key_grads.shape[1]
    smem, vmem = (pl.BlockSpec(memory_space=space) for space in (pltpu.SMEM, pltpu.VMEM))
    return call(
        functools.partial(grad_kernel, block=block),
        pltpu.VMEM((depth // 2, features), dtype),
        flops=len(xs) * depth * rows * features,
        in_specs=[smem, smem] + [vmem] * (len(xs) + 1),
        out_specs=vmem,
    )(half.reshape(1), zl.reshape(1), *xs, key_grads)


def inner_kernel(s_ref, o_ref, w_ref, out_ref):
    ny, nx, nz, own, _ = out_ref.shape
    for y in range(ny):
        rows = pl.ds(y * nz * nx * own, nz * nx * own)
        grad = s_ref[rows] + o_ref[rows].astype(F32)
        local = (w_ref[rows].astype(F32) - ETA * grad).astype(BF)
        for z in range(nz):
            for x in range(nx):
                start = (z * nx + x) * own
                out_ref[y, x, z] = local[start : start + own]


def inner_step(same, other, w):
    rows, features = w.shape
    ny, nz, nx = SIZES[:3]
    return call(
        inner_kernel,
        pltpu.VMEM((ny, nx, nz, rows // (ny * nz * nx), features), BF),
        moved=8 * w.size,
        in_specs=[pl.BlockSpec(memory_space=pltpu.VMEM)] * 3,
        out_specs=pl.BlockSpec(memory_space=pltpu.VMEM),
    )(same, other, w)


def total_kernel(zh_ref, l_ref, held_ref, out_ref, low_ref):
    own = held_ref.shape[2]
    total = l_ref[0].astype(F32)
    for i in range(1, l_ref.shape[0]):
        total += l_ref[i].astype(F32)
    out_ref[...] = total
    low_ref[...] = total.astype(BF)
    rows = pl.ds(pl.multiple_of(zh_ref[0] * own, own), own)
    from_base = (1.0 - SHARE) * held_ref[0, 0] - OUTER_RATE * MOMENT * MOMENT * held_ref[1, 0]
    low_ref[rows] = (out_ref[rows] + from_base * (N_REP / SHARE)).astype(BF)


def half_total(zh, shares, held):
    shape = shares.shape[1:]
    smem, vmem = (pl.BlockSpec(memory_space=space) for space in (pltpu.SMEM, pltpu.VMEM))
    return call(
        total_kernel,
        (jax.ShapeDtypeStruct(shape, F32), jax.ShapeDtypeStruct(shape, BF)),
        in_specs=[smem, vmem, vmem],
        out_specs=(vmem,) * 2,
    )(zh.reshape(1), shares, held)


def outer_kernel(zh_ref, s_ref, o_ref, held_ref, base_ref, mom_ref, all_ref):
    own = held_ref.shape[2]
    rows = pl.ds(pl.multiple_of(zh_ref[0] * own, own), own)
    partner_rows = pl.ds(pl.multiple_of((1 - zh_ref[0]) * own, own), own)
    partner = 1 - zh_ref[0]
    average = (s_ref[rows] + o_ref[partner, rows].astype(F32)) / N_REP
    base = held_ref[0, 0]
    delta = base - average
    new_mom = MOMENT * held_ref[1, 0] + delta
    new_base = base - OUTER_RATE * (delta + MOMENT * new_mom)
    mom_ref[0] = new_mom
    base_ref[0] = new_base
    low = new_base.astype(BF)
    partner_low = ((s_ref[partner_rows] + o_ref[partner, partner_rows].astype(F32)) * (SHARE / N_REP)).astype(BF)
    for i in range(all_ref.shape[0]):
        all_ref[i, rows] = low
        all_ref[i, partner_rows] = partner_low


def outer_step(zh, total, other, held, n):
    smem, vmem = (pl.BlockSpec(memory_space=space) for space in (pltpu.SMEM, pltpu.VMEM))
    shape = jax.ShapeDtypeStruct(held.shape[1:], F32)
    return call(
        outer_kernel,
        (shape, shape, jax.ShapeDtypeStruct((n, *total.shape), BF)),
        in_specs=[smem] + [vmem] * 3,
        out_specs=(vmem,) * 3,
    )(zh.reshape(1), total, other, held)


def hold_kernel(a_ref, m_ref, out_ref):
    out_ref[0] = a_ref[...]
    out_ref[1] = m_ref[...]


def hold(anchor, momentum):
    return call(hold_kernel, pltpu.VMEM((2, *anchor.shape), F32))(anchor, momentum)


def mix_kernel(l_ref, b_ref, out_ref, lh_ref, held_ref, sems):
    ny, nx, nz, own, _ = b_ref.shape
    rows = nz * nx * own
    reads = [pltpu.make_async_copy(l_ref.at[y], lh_ref.at[y], sems.at[0, y]) for y in range(ny)]
    for copy in reads:
        copy.start()
    writes = []
    for y in range(ny):
        reads[y].wait()
        mixed = (1.0 - MIX_RATE) * lh_ref[y].astype(F32) + MIX_RATE * b_ref[y].astype(F32)
        mixed = mixed.astype(BF)
        for z in range(nz):
            for x in range(nx):
                held_ref[pl.ds(((y * nz + z) * nx + x) * own, own)] = mixed[x, z]
        part = pl.ds(y * rows, rows)
        writes.append(pltpu.make_async_copy(held_ref.at[part], out_ref.at[0, part], sems.at[1, y]))
        writes[-1].start()
    for copy in writes:
        copy.wait()


def mix(local, base):
    ny, nx, nz, own, features = local.shape
    rows = ny * nx * nz * own
    return call(
        mix_kernel,
        jax.ShapeDtypeStruct((1, rows, features), BF),
        in_specs=[pl.BlockSpec(memory_space=pl.ANY), pl.BlockSpec(memory_space=pltpu.VMEM)],
        out_specs=pl.BlockSpec(memory_space=pl.ANY),
        scratch_shapes=[
            pltpu.VMEM(local.shape, BF),
            pltpu.VMEM((rows, features), BF),
            pltpu.SemaphoreType.DMA((2, ny)),
        ],
    )(local, base)


def across(value, axis, k):
    return lax.ppermute(value, axis, [(i, i ^ k) for i in range(4)])


def body(tokens, cotangent, local_weights, anchor, momentum):
    own = local_weights[0]
    depth, features = own.shape
    width = tokens.shape[1] // SIZES[3]
    core, zl, zh = (lax.axis_index(name) for name in ("core", "zl", "zh"))
    got = [None] + [across(x, "zl", k) for k, x in zip((1, 2, 3), slices(zl, tokens, (1, 2, 3)))]
    swapped = lax.ppermute(own, "core", SWAP)
    held = hold(anchor, momentum)
    (got[0],) = slices(zl, tokens, (0,))
    got[0], held = lax.optimization_barrier((got[0], held))
    parts = [project(core, got[0], own, swapped)]
    turned = [flip(got[0])]
    got[2], got[1], parts, turned = lax.optimization_barrier((got[2], got[1], parts, turned))
    for k, before in ((2, None), (1, 2), (3, 1)):
        if before:
            got[k], made = lax.optimization_barrier((got[k], made))
        made = project(core, got[k], own, swapped)
        parts.append(across(made, "zl", k))
    parts[1], parts[2] = parts[2], parts[1]
    got, made = lax.optimization_barrier((got, made))
    turned += [flip(x) for x in got[1:]]
    parts, turned = lax.optimization_barrier((parts, turned))
    key_grad = norm_grad(parts, cotangent)
    key_grads = lax.all_gather(key_grad, "zl", axis=0, tiled=True)
    send = gradient(1 - core, zl, turned, key_grads, BF)
    same = gradient(core, zl, turned, key_grads, F32)
    local = inner_step(same, lax.ppermute(send, "core", SWAP), own)
    ny, nx, nz, rows, _ = local.shape
    shares = lax.all_to_all(local.reshape(ny * nx, nz * rows, features), ("y", "x"), 0, 0, tiled=True)
    total, low = half_total(zh, shares, held)
    both = lax.all_gather(low, "zh")
    new_base, new_mom, spread = outer_step(zh, total, both, held, ny * nx)
    base = lax.all_to_all(spread, ("y", "x"), 0, 0, tiled=True).reshape(local.shape)
    return mix(local, base), new_base, new_mom


def solution(mesh):
    fine = Mesh(mesh.devices.reshape(SIZES), AXES)
    placed = (
        P((*REP, *FSDP), None),
        P((*REP, *FSDP), None),
        P(REP, FSDP, None),
        P(FSDP, REP, None),
        P(FSDP, REP, None),
    )
    return jax.shard_map(
        body,
        mesh=fine,
        in_specs=placed,
        out_specs=(P(REP, FSDP, None), P(FSDP, REP, None), P(FSDP, REP, None)),
        check_vma=False,
    )
```
